1024 devices in a mesh: table: 64 (over z, core), bal: 16 (over x, y).
Axes of the slice: x: 4, y: 4, z: 32, core: 2. Of those that a mesh axis runs over, the one named last changes fastest.
Arguments:
- item_ids: int32 [262144], P(('table', 'bal')), may hold values from 0 to 65535, as said below
- hot_slot: int32 [65536], replicated, may hold values from 0 to 1024, as said below
- hot_rows: bfloat16 [1024, 512], replicated, may hold values from -6 to 6
- cold_rows: bfloat16 [65536, 512], P('table'), may hold values from -6 to 6
- hist_lengths: int32 [2048], replicated, may hold values from 1 to 128
- out_grad: bfloat16 [262144, 512], P(('table', 'bal')), may hold values from -6 to 6
- w_uvqk: bfloat16 [512, 2048], replicated, may hold values from -0.25 to 0.25
- w_out: bfloat16 [512, 512], replicated, may hold values from -0.25 to 0.25
Outputs:
- layer_out: bfloat16 [262144, 512], P(('table', 'bal'))
- grad_uvqk: float32 [32768, 2048], P(('table', 'bal'))
- grad_out_proj: float32 [32768, 512], P(('table', 'bal'))
The draws below stay inside these ranges and needn't reach their ends.
Inputs may be any that keep to these rules, and one draw needn't show every extreme that they name: `item_ids`: item i lies in table shard i // 1024. In each device's block of 256 token slots at most 4 tokens with cold items name items of one shard, and some shard gets exactly 4 of them in every block. `hot_slot`: each value below 1024 is taken by exactly one item; 1024 marks a cold item.
All inputs are finite; a program needn't handle non-finite values.
Results may differ from the reference program's by a relative error of at most 0.012.
Values may be sent and summed in bfloat16 or wider, within the bound.
A program may use at most 64 MiB of HBM per device.

```python
import math
import jax
import jax.numpy as jnp
from jax import lax

D = 512
HEADS = 4
MAXLEN = 128
USR_DEV = 2
ROWS_DEV = 1024
HOT = 1024
TOK_DEV = 256
USERS = 2048
TOKENS = 262144
ITEMS = 65536
N_TABLE = 64
N_BAL = 16


def hot_list(key):
    half_rows = ROWS_DEV // 2
    owner_count = ITEMS // ROWS_DEV
    chosen = jax.random.permutation(jax.random.fold_in(key, 7), owner_count * half_rows)[:HOT]
    return (chosen // half_rows * ROWS_DEV + chosen % half_rows).astype(jnp.int32)


def draw_hot_slot(key, part):
    hot_items = hot_list(key)
    return jnp.full((ITEMS,), HOT, jnp.int32).at[hot_items].set(jnp.arange(HOT, dtype=jnp.int32))


def draw_item_ids(key, part):
    half_rows = ROWS_DEV // 2
    owner_count = ITEMS // ROWS_DEV
    block_count = TOKENS // TOK_DEV
    hot_items = hot_list(key)
    key_perm, key_forced, key_coin, key_hot, key_cold = jax.random.split(jax.random.fold_in(key, 11), 5)
    shuffles = jax.vmap(lambda one_key: jax.random.permutation(one_key, TOK_DEV))(jax.random.split(key_perm, block_count))
    owner_of = (shuffles % owner_count).astype(jnp.int32)
    forced_owner = jax.random.randint(key_forced, (block_count, 1), 0, owner_count)
    coin_flip = jax.random.randint(key_coin, (block_count, TOK_DEV), 0, 2)
    use_hot = (coin_flip == 1) & (owner_of != forced_owner)
    hot_pick = hot_items[jax.random.randint(key_hot, (block_count, TOK_DEV), 0, HOT)]
    cold_pick = owner_of * ROWS_DEV + half_rows + jax.random.randint(key_cold, (block_count, TOK_DEV), 0, ROWS_DEV - half_rows)
    return jnp.where(use_hot, hot_pick, cold_pick).astype(jnp.int32).reshape(TOKENS)


def plant(values, rng, least, high):
    spot = [jax.random.randint(jax.random.fold_in(rng, axis), (), 0, length) for axis, length in enumerate(values.shape)]
    widest = values.shape.index(max(values.shape))
    beside = spot[:widest] + [(spot[widest] + 1) % values.shape[widest]] + spot[widest + 1:]
    return values.at[tuple(spot)].set(least).at[tuple(beside)].set(high)


def level_of(stream_key, extent, cuts, low, high):
    def one(dim, shards_of):
        heights = jax.random.uniform(jax.random.fold_in(jax.random.fold_in(stream_key, 6), dim), (shards_of,), jnp.float32, low / len(cuts), high / len(cuts))
        return jnp.repeat(jnp.exp(heights), extent[dim] // shards_of).reshape((-1,) + (1,) * (len(extent) - dim - 1))

    gain = one(*cuts[0])
    for cut in cuts[1:]:
        gain = gain * one(*cut)
    return gain


def normal_values(key, dims, width, most, shards=(), kind=jnp.bfloat16):
    gain = level_of(key, dims, shards, -0.22, 0.18) if shards else 1.0
    result = jax.random.normal(key, dims, jnp.float32) * width * gain
    return jnp.minimum(jnp.maximum(result, -most), most).astype(kind)


def setup_inputs(seed: int = 0) -> dict:
    keys = jax.random.split(jax.random.key(seed), 9)
    return {
        "item_ids": draw_item_ids(jax.random.fold_in(keys[8], 71), 0),
        "hot_slot": draw_hot_slot(jax.random.fold_in(keys[8], 71), 0),
        "hot_rows": normal_values(keys[2], (HOT, D), 1.0, 6.0),
        "cold_rows": normal_values(keys[3], (ITEMS, D), 1.0, 6.0, ((0, 64),)),
        "hist_lengths": plant(jax.random.randint(keys[4], (USERS,), 1, MAXLEN + 1), jax.random.fold_in(keys[4], 1), 1, MAXLEN).astype(jnp.int32),
        "out_grad": normal_values(keys[5], (TOKENS, D), 1.0, 6.0, ((0, 1024),)),
        "w_uvqk": normal_values(keys[6], (D, 4 * D), D ** -0.5, 0.25),
        "w_out": normal_values(keys[7], (D, D), D ** -0.5, 0.25),
    }


def norm_rows(values_in):
    average = lax.optimization_barrier(jnp.mean(values_in, axis=-1, keepdims=True))
    centred = values_in - average
    spread = lax.optimization_barrier(jnp.mean(centred * centred, axis=-1, keepdims=True))
    return centred * lax.rsqrt(spread + 1e-05)

def attend(hidden, length):
    row_count = hidden.shape[0]
    features = hidden.shape[1] // 4
    head_size = features // HEADS
    activated = jax.nn.silu(hidden)
    gate_part = activated[:, :features].astype(jnp.bfloat16)
    value_part = activated[:, features:2 * features].astype(jnp.bfloat16)
    query_part = activated[:, 2 * features:3 * features].astype(jnp.bfloat16)
    key_part = activated[:, 3 * features:].astype(jnp.bfloat16)
    query_heads = query_part.reshape(row_count, HEADS, head_size).astype(jnp.float32)
    key_heads = key_part.reshape(row_count, HEADS, head_size).astype(jnp.float32)
    value_heads = value_part.reshape(row_count, HEADS, head_size).astype(jnp.float32)
    scores = jnp.einsum('ihe,jhe->hij', query_heads, key_heads) * (1.0 / math.sqrt(head_size))
    position = jnp.arange(row_count, dtype=jnp.int32)
    allowed = (position[None, :] <= position[:, None]) & (position[:, None] < length)
    weights = jnp.where(allowed[None], jax.nn.silu(scores), 0.0).astype(jnp.bfloat16)
    mixed = jnp.einsum('hij,jhe->ihe', weights.astype(jnp.float32), value_heads).reshape(row_count, features)
    return (norm_rows(mixed) * gate_part.astype(jnp.float32)).astype(jnp.bfloat16)

def user_pass(user_emb, user_cot, length, w_uvqk, w_out, grad_scale):
    row_count = user_emb.shape[0]
    normed = norm_rows(user_emb.astype(jnp.float32)).astype(jnp.bfloat16)
    hidden = jnp.dot(normed, w_uvqk, preferred_element_type=jnp.float32)
    gated, pullback = jax.vjp(lambda hidden_in: attend(hidden_in, length), hidden)
    output = (user_emb.astype(jnp.float32) + jnp.dot(gated, w_out, preferred_element_type=jnp.float32)).astype(jnp.bfloat16)
    is_valid = jnp.arange(row_count, dtype=jnp.int32) < length
    signal = (jnp.where(is_valid[:, None], user_cot.astype(jnp.float32), 0.0) * grad_scale).astype(jnp.bfloat16)
    back_signal = jnp.dot(signal, w_out.T, preferred_element_type=jnp.float32).astype(jnp.bfloat16)
    grad_hidden = pullback(back_signal)[0].astype(jnp.bfloat16)
    grad_first = jnp.einsum('td,tf->df', normed.astype(jnp.float32), grad_hidden.astype(jnp.float32))
    grad_second = jnp.einsum('td,tf->df', gated.astype(jnp.float32), signal.astype(jnp.float32))
    return (output, grad_first, grad_second)

def reference(item_ids, hot_slot, hot_rows, cold_rows, hist_lengths, out_grad, w_uvqk, w_out):
    hot_index = hot_slot[item_ids]
    is_hot = hot_index < HOT
    embedded = jnp.where(is_hot[:, None], hot_rows[jnp.minimum(hot_index, HOT - 1)], cold_rows[item_ids])
    group_users = N_BAL * USR_DEV
    grad_scale = 1.0 / math.sqrt(N_BAL * USR_DEV * MAXLEN)
    grouped = embedded.reshape(N_TABLE, group_users, MAXLEN, D)
    cotangent = out_grad.reshape(N_TABLE, group_users, MAXLEN, D)
    lengths = hist_lengths.reshape(N_TABLE, group_users)

    def per_group(inputs):

        def per_user(running, pieces):
            output, grad_first, grad_second = user_pass(pieces[0], pieces[1], pieces[2], w_uvqk, w_out, grad_scale)
            return ((running[0] + grad_first, running[1] + grad_second), output)
        initial = (jnp.zeros((D, 4 * D), jnp.float32), jnp.zeros((D, D), jnp.float32))
        totals, outputs = lax.scan(per_user, initial, inputs)
        return (outputs, totals[0], totals[1])
    outputs, grad_first, grad_second = lax.map(per_group, (grouped, cotangent, lengths))
    return (outputs.reshape(TOKENS, D), grad_first.reshape(N_TABLE * D, 4 * D), grad_second.reshape(N_TABLE * D, D))
```

```python
import functools
import math

import jax
import jax.numpy as jnp
from jax import lax
from jax.experimental import pallas as pl
from jax.experimental.pallas import tpu as pltpu
from jax.sharding import PartitionSpec as P

HEADS = 4
MAXLEN = 128
HALF = 1280
BF, F32 = jnp.bfloat16, jnp.float32
VMEM = pl.BlockSpec(memory_space=pltpu.VMEM)
SMEM = pl.BlockSpec(memory_space=pltpu.SMEM)


def dot(a, b, ca=1, cb=0):
    return lax.dot_general(a, b, (((ca,), (cb,)), ((), ())), preferred_element_type=F32)


def iota(shape, dim):
    return lax.broadcasted_iota(jnp.int32, shape, dim)


def one_hot(cond):
    return jnp.where(cond, 1.0, 0.0).astype(BF)


def each_peer(n, me, do):
    do(lax.rem(me + n // 2, n))

    def both(i, _):
        away = n // 2 - 1 - i
        do(lax.rem(me + away, n))
        do(lax.rem(me + n - away, n))
        return 0

    lax.fori_loop(0, n // 2 - 1, both, 0)


def lookup_kernel(
    n, ids_ref, slot_ref, hot_ref, cold_ref, emb_ref,
    ask, asked, wide, found, reply, barely, send_sem, recv_sem,
):
    me = lax.axis_index("table")
    barrier = pltpu.get_barrier_semaphore()

    def greet(peer):
        pl.semaphore_signal(barrier, inc=1, device_id={"table": peer}, device_id_type=pl.DeviceIdType.MESH)

    each_peer(n, me, greet)

    tokens = ids_ref.shape[1]
    per = tokens // n
    shard = cold_ref.shape[0]
    hot_count = hot_ref.shape[0]
    ids_row = jnp.broadcast_to(ids_ref[...].astype(F32), (tokens, tokens))
    diag = iota((tokens, tokens), 0) == iota((tokens, tokens), 1)
    ids = jnp.sum(jnp.where(diag, ids_row, 0.0), axis=1, keepdims=True).astype(jnp.int32)
    lines = slot_ref.shape[0]
    pick = one_hot(iota((tokens, lines), 1) == ids // 128)
    slots = slot_ref[...]
    high = dot(pick, (slots // 8).astype(F32).astype(BF))
    low = dot(pick, (slots % 8).astype(F32).astype(BF))
    lane = iota((tokens, 128), 1)
    hot_index = jnp.sum(jnp.where(lane == ids % 128, high * 8.0 + low, 0.0), axis=1, keepdims=True).astype(jnp.int32)
    owner = ids // shard
    row = ids % shard
    cold = hot_index >= hot_count
    marks = one_hot((lane == owner) & cold)
    before = dot(one_hot(iota((tokens, tokens), 1) < iota((tokens, tokens), 0)), marks)
    place = jnp.sum(before * marks.astype(F32), axis=1, keepdims=True).astype(jnp.int32)
    digits = jnp.where(
        lane == place, (row // 8).astype(F32), jnp.where(lane == place + per, (row % 8).astype(F32), 0.0)
    ).astype(BF)
    ask[...] = dot(marks, digits, 0, 0)[:n].reshape(n, 1, 128)

    pl.semaphore_wait(barrier, n - 1)

    def send(src, dst, k):
        def one(peer):
            pltpu.make_async_remote_copy(
                src_ref=src.at[peer], dst_ref=dst.at[me], send_sem=send_sem.at[k], recv_sem=recv_sem.at[k],
                device_id={"table": peer}, device_id_type=pl.DeviceIdType.MESH,
            ).start()

        each_peer(n, me, one)

    def settle(ref, sem):
        part = ref.at[pl.ds(0, n - 1)]
        pltpu.make_async_copy(part, part, sem).wait()

    send(ask, asked, 0)
    asked[me] = ask[me]
    hot_part = dot(one_hot(iota((tokens, hot_count), 1) == hot_index), hot_ref[...])
    settle(asked, recv_sem.at[0])

    spread = one_hot(iota((tokens, n), 0) // per == iota((tokens, n), 1))
    got = dot(spread, asked[...].reshape(n, 128).astype(BF))
    turn = iota((tokens, 128), 0) % per
    want = jnp.sum(
        jnp.where(lane == turn, got * 8.0, jnp.where(lane == turn + per, got, 0.0)), axis=1, keepdims=True
    ).astype(jnp.int32)
    rows = dot(one_hot(iota((tokens, shard), 1) == want), cold_ref[...])
    pieces = rows.shape[1] // 128
    for j in range(pieces):
        wide[pl.ds(j, tokens, stride=pieces), :] = rows[:, j * 128 : (j + 1) * 128]
    found[...] = wide[...].astype(BF).reshape(found.shape)
    send(found, reply, 1)
    reply[me] = found[me]
    barely[...] = hot_part
    slot = jnp.where(cold, owner * per + place, -1)
    settle(reply, recv_sem.at[1])

    wide[...] = reply[...].reshape(wide.shape).astype(F32)
    take = one_hot(iota((tokens, tokens), 1) == slot)
    for j in range(pieces):
        cut = slice(j * 128, (j + 1) * 128)
        piece = wide[pl.ds(j, tokens, stride=pieces), :].astype(BF)
        emb_ref[:, cut] = (barely[:, cut] + dot(take, piece)).astype(BF)
    settle(ask, send_sem.at[0])
    settle(found, send_sem.at[1])


def lookup(n, ids, hot_slot, hot_rows, cold_rows):
    tokens = ids.shape[0]
    features = hot_rows.shape[1]
    piece = features // 128 * (tokens // n)
    return pl.pallas_call(
        functools.partial(lookup_kernel, n),
        out_shape=jax.ShapeDtypeStruct((tokens, features), BF),
        in_specs=[VMEM] * 4,
        out_specs=VMEM,
        scratch_shapes=[
            pltpu.VMEM((n, 1, 128), F32),
            pltpu.VMEM((n, 1, 128), F32),
            pltpu.VMEM((n * piece, 128), F32),
            pltpu.VMEM((n, piece, 128), BF),
            pltpu.VMEM((n, piece, 128), BF),
            pltpu.VMEM((tokens, features), F32),
            pltpu.SemaphoreType.DMA((2,)),
            pltpu.SemaphoreType.DMA((2,)),
        ],
        compiler_params=pltpu.CompilerParams(
            collective_id=0, has_side_effects=True, vmem_limit_bytes=40 * 2**20
        ),
        name="lookup",
    )(ids.reshape(1, tokens), hot_slot.reshape(-1, 128), hot_rows, cold_rows)


def normalised(values):
    mean = jnp.mean(values, axis=-1, keepdims=True)
    centred = values - mean
    scale = lax.rsqrt(jnp.mean(centred * centred, axis=-1, keepdims=True) + 1e-05)
    return centred * scale, scale


def silu_both(v):
    sig = 0.5 * jnp.tanh(0.5 * v) + 0.5
    act = v * sig
    return act, sig + act * (1.0 - sig)


def layer_kernel(
    grad_scale, len_ref, emb_ref, cot_ref, wu_ref, wo_ref, out_ref, grad_ref,
    slope, acts, attn, attn_slope, mixed, grads,
):
    tokens, features = emb_ref.shape
    users = tokens // MAXLEN
    head = features // HEADS
    first = (lax.axis_index("table") * lax.axis_size("bal") + lax.axis_index("bal")) * users
    lengths = [len_ref[first + u] for u in range(users)]
    emb = emb_ref[...].astype(F32)
    normed = normalised(emb)[0].astype(BF)
    for b in range(4):
        cut = slice(b * features, (b + 1) * features)
        act, dact = silu_both(dot(normed, wu_ref[:, cut]))
        acts[:, cut] = act.astype(BF)
        slope[:, cut] = dact
    i, j = iota((MAXLEN, MAXLEN), 0), iota((MAXLEN, MAXLEN), 1)
    scale = 1.0 / math.sqrt(head)

    def part(b, u, h):
        at = b * features + h * head
        return acts[u * MAXLEN : (u + 1) * MAXLEN, at : at + head]

    for u in range(users):
        allowed = (j <= i) & (i < lengths[u])
        for h in range(HEADS):
            s = dot(part(2, u, h), part(3, u, h), 1, 1) * scale
            act, dact = silu_both(s)
            w = jnp.where(allowed, act, 0.0).astype(BF)
            attn[u * HEADS + h] = w
            attn_slope[u * HEADS + h] = jnp.where(allowed, dact * scale, 0.0)
            mixed[u * MAXLEN : (u + 1) * MAXLEN, h * head : (h + 1) * head] = dot(w, part(1, u, h))

    n, rstd = normalised(mixed[...])
    gate = acts[:, :features].astype(F32)
    gated = (n * gate).astype(BF)
    out_ref[...] = (emb + dot(gated, wo_ref[...])).astype(BF)
    at = iota((tokens, 1), 0)
    ends = jnp.full((tokens, 1), lengths[0], jnp.int32)
    for u in range(1, users):
        ends = jnp.where(at >= u * MAXLEN, u * MAXLEN + lengths[u], ends)
    valid = at < ends
    signal = (jnp.where(valid, cot_ref[...].astype(F32), 0.0) * grad_scale).astype(BF)
    back = dot(signal, wo_ref[...], 1, 1).astype(BF).astype(F32)
    dn = back * gate
    dmixed = rstd * (
        dn - jnp.mean(dn, axis=-1, keepdims=True) - n * jnp.mean(dn * n, axis=-1, keepdims=True)
    )
    mixed[...] = dmixed
    grads[:, :features] = ((back * n).astype(BF).astype(F32) * slope[:, :features]).astype(BF)
    for u in range(users):
        rows = slice(u * MAXLEN, (u + 1) * MAXLEN)
        for h in range(HEADS):
            dm = mixed[rows, h * head : (h + 1) * head].astype(BF)
            w = attn[u * HEADS + h]
            dw = dot(dm, part(1, u, h), 1, 1).astype(BF).astype(F32)
            ds = (dw * attn_slope[u * HEADS + h]).astype(BF)
            for b, d in (
                (1, dot(w, dm, 0, 0)),
                (2, dot(ds, part(3, u, h))),
                (3, dot(ds, part(2, u, h), 0, 0)),
            ):
                cols = slice(b * features + h * head, b * features + (h + 1) * head)
                grads[rows, cols] = (d.astype(BF).astype(F32) * slope[rows, cols]).astype(BF)

    across = 256
    height = features // 16
    for c in range(0, 4 * features, across):
        emit(grad_ref, dot(normed, grads[:, c : c + across], 0, 0).astype(BF), c, height)
    for c in range(0, features, across):
        emit(grad_ref, dot(gated, signal[:, c : c + across], 0, 0).astype(BF), 4 * features + c, height)


def emit(grad_ref, value, column, height):
    half, at = divmod(column, HALF)
    for b in range(16):
        x, y = divmod(b, 4)
        f, s = (x, y) if half == 0 else (y, x)
        grad_ref[half, f, s, :, at : at + value.shape[1]] = value[b * height : (b + 1) * height]


def layer(grad_scale, lengths, emb, cot, wu, wo):
    tokens, features = emb.shape
    users = tokens // MAXLEN
    return pl.pallas_call(
        functools.partial(layer_kernel, grad_scale),
        out_shape=(
            jax.ShapeDtypeStruct((tokens, features), BF),
            jax.ShapeDtypeStruct((2, 4, 4, features // 16, HALF), BF),
        ),
        in_specs=[SMEM] + [VMEM] * 4,
        out_specs=(VMEM, VMEM),
        scratch_shapes=[
            pltpu.VMEM((tokens, 4 * features), F32),
            pltpu.VMEM((tokens, 4 * features), BF),
            pltpu.VMEM((users * HEADS, MAXLEN, MAXLEN), BF),
            pltpu.VMEM((users * HEADS, MAXLEN, MAXLEN), F32),
            pltpu.VMEM((tokens, features), F32),
            pltpu.VMEM((tokens, 4 * features), BF),
        ],
        compiler_params=pltpu.CompilerParams(vmem_limit_bytes=48 * 2**20),
        name="layer",
    )(lengths, emb, cot, wu, wo)


def reduce_kernel(
    g, first_ref, second_ref, in1, out1, total, tot_bf, in2, out2, send1, recv1, send2, recv2
):
    me = lax.axis_index("bal")
    x, y = me // 4, me % 4

    def along_x(step):
        return (x + step) % 4 * 4 + y

    def along_y(step):
        return x * 4 + (y + step) % 4

    def copy(src, dst, send_sem, recv_sem, peer):
        return pltpu.make_async_remote_copy(
            src_ref=src, dst_ref=dst, send_sem=send_sem, recv_sem=recv_sem,
            device_id={"bal": peer}, device_id_type=pl.DeviceIdType.MESH,
        )

    barrier = pltpu.get_barrier_semaphore()
    for peer in (along_x(1), along_x(3), along_y(1), along_y(3)):
        pl.semaphore_signal(barrier, inc=1, device_id={"bal": peer}, device_id_type=pl.DeviceIdType.MESH)
    pl.semaphore_wait(barrier, 4)

    ways = [(half, way) for half in range(2) for way in range(2)]
    steps = (1, 3)
    places = ((x, y), (y, x))
    moves = ((along_x, along_y), (along_y, along_x))
    copies = []

    def stage1(half, way, msg):
        a = places[half][0]
        mine, other = pl.ds(2 * way, 2), pl.ds(2 - 2 * way, 2)
        src = (
            g.at[half, (a + 2) % 4, mine],
            g.at[half, (a + steps[way]) % 4, other],
            out1.at[half, way],
        )[msg]
        c = copy(
            src, in1.at[half, way, msg], send1.at[half, way, msg], recv1.at[half, way, msg],
            moves[half][0](steps[way]),
        )
        c.start()
        return c

    sent = {}
    for msg in (0, 1):
        for half, way in ways:
            sent[half, way, msg] = stage1(half, way, msg)
    for half, way in ways:
        a = places[half][0]
        sent[half, way, 0].wait_recv()
        own = g[half, (a + steps[way]) % 4, pl.ds(2 * way, 2)]
        out1[half, way] = (own.astype(F32) + in1[half, way, 0].astype(F32)).astype(BF)
        sent[half, way, 2] = stage1(half, way, 2)

    height = first_ref.shape[0]
    mid = height // 2

    def stage2(half, way, msg):
        b = places[half][1]
        mine, other = pl.ds(mid * way, mid), pl.ds(mid - mid * way, mid)
        src = (
            tot_bf.at[half, (b + 2) % 4, mine],
            tot_bf.at[half, (b + steps[way]) % 4, other],
            out2.at[half, way],
        )[msg]
        c = copy(
            src, in2.at[half, way, msg], send2.at[half, way, msg], recv2.at[half, way, msg],
            moves[half][1](steps[way]),
        )
        c.start()
        return c

    later = {}
    for half in range(2):
        a = places[half][0]
        for way in range(2):
            sent[half, way, 1].wait_recv()
            sent[half, way, 2].wait_recv()
        for part in range(2):
            here = pl.ds(2 * part, 2)
            t = (
                g[half, a, here].astype(F32)
                + in1[half, part, 2].astype(F32)
                + in1[half, 1 - part, 1].astype(F32)
            )
            total[half, here] = t
            tot_bf[half, here] = t.astype(BF)
        for msg in (0, 1):
            for way in range(2):
                later[half, way, msg] = stage2(half, way, msg)
    for half, way in ways:
        b = places[half][1]
        later[half, way, 0].wait_recv()
        own = total[half, (b + steps[way]) % 4, pl.ds(mid * way, mid)]
        out2[half, way] = (own + in2[half, way, 0].astype(F32)).astype(BF)
        later[half, way, 2] = stage2(half, way, 2)
    split = first_ref.shape[1] - HALF
    for half in range(2):
        b = places[half][1]
        for way in range(2):
            later[half, way, 1].wait_recv()
            later[half, way, 2].wait_recv()
        for part in range(2):
            rows = pl.ds(mid * part, mid)
            t = (
                total[half, b, rows]
                + in2[half, part, 2].astype(F32)
                + in2[half, 1 - part, 1].astype(F32)
            )
            if half == 0:
                first_ref[rows, :HALF] = t
            else:
                first_ref[rows, HALF:] = t[:, :split]
                second_ref[rows, :] = t[:, split:]
    for c in (*sent.values(), *later.values()):
        c.wait_send()


def reduce(g, features):
    height = features // 16
    dma = pltpu.SemaphoreType.DMA((2, 2, 3))
    return pl.pallas_call(
        reduce_kernel,
        out_shape=(
            jax.ShapeDtypeStruct((height, 4 * features), F32),
            jax.ShapeDtypeStruct((height, features), F32),
        ),
        in_specs=[VMEM],
        out_specs=(VMEM, VMEM),
        scratch_shapes=[
            pltpu.VMEM((2, 2, 3, 2, height, HALF), BF),
            pltpu.VMEM((2, 2, 2, height, HALF), BF),
            pltpu.VMEM((2, 4, height, HALF), F32),
            pltpu.VMEM((2, 4, height, HALF), BF),
            pltpu.VMEM((2, 2, 3, height // 2, HALF), BF),
            pltpu.VMEM((2, 2, height // 2, HALF), BF),
            dma, dma, dma, dma,
        ],
        compiler_params=pltpu.CompilerParams(
            collective_id=1, has_side_effects=True, vmem_limit_bytes=40 * 2**20
        ),
        name="reduce",
    )(g)


def per_device(item_ids, hot_slot, hot_rows, cold_rows, hist_lengths, out_grad, w_uvqk, w_out):
    tokens, features = out_grad.shape
    grad_scale = 1.0 / math.sqrt(lax.axis_size("bal") * tokens)
    emb = lookup(lax.axis_size("table"), item_ids, hot_slot, hot_rows, cold_rows)
    layer_out, g = layer(grad_scale, hist_lengths, emb, out_grad, w_uvqk, w_out)
    return (layer_out, *reduce(g, features))


def solution(mesh):
    both = P(("table", "bal"), None)
    return jax.shard_map(
        per_device,
        mesh=mesh,
        in_specs=(P(("table", "bal")), P(), P(), P("table", None), P(), both, P(), P()),
        out_specs=(both, both, both),
        check_vma=False,
    )
```

```python
import functools
import math

import jax
import jax.numpy as jnp
from jax import lax
from jax.experimental import pallas as pl
from jax.experimental.pallas import tpu as pltpu
from jax.sharding import PartitionSpec as P

HEADS = 4
MAXLEN = 128
BF, F32 = jnp.bfloat16, jnp.float32
VMEM = pl.BlockSpec(memory_space=pltpu.VMEM)
HBM = pl.BlockSpec(memory_space=pltpu.HBM)


def dot(a, b, ca=1, cb=0):
    return lax.dot_general(a, b, (((ca,), (cb,)), ((), ())), preferred_element_type=F32)


def iota(shape, dim):
    return lax.broadcasted_iota(jnp.int32, shape, dim)


def one_hot(cond):
    return jnp.where(cond, 1.0, 0.0).astype(BF)


def at_distance(z_count, me, d, do):
    z, core = me // 2, me % 2
    for step, rank, mirrored in ((d, 2 * d - 1, 2 * d), (z_count - d, 2 * d, 2 * d - 1)):
        for c in range(2):
            do(lax.rem(z + step, z_count) * 2 + c, rank * 2 + c, mirrored * 2 + core)


def in_range(z_count, me, low, high, do):
    z, core = me // 2, me % 2
    if high == z_count // 2:
        for c in range(2):
            do(lax.rem(z + high, z_count) * 2 + c, (z_count - 1) * 2 + c, (z_count - 1) * 2 + core)
        high -= 1
    least = max(low, 1)

    def one(i, _):
        at_distance(z_count, me, high - i, do)
        return 0

    lax.fori_loop(0, high - least + 1, one, 0)
    if low == 0:
        do(z * 2 + 1 - core, 1 - core, core)


def ranges(z_count):
    ends = [z_count // 8 - 1, z_count // 4 - 1, 3 * z_count // 8 - 1, z_count // 2]
    low, first, out = 0, 0, []
    for high in ends:
        last = 2 * z_count if high == z_count // 2 else 4 * high + 2
        out.append((low, high, first, last))
        low, first = high + 1, last
    return out


def lookup(
    n, loads, near, meanwhile, ids_ref, slot_ref, hot_ref, cold_ref, ask, asked, wide, found, reply, emb_ref,
    ask_send, ask_recv, reply_send, reply_recv,
):
    z_count = n // 2
    me = lax.axis_index("table")
    z, core = me // 2, me % 2
    batches = ranges(z_count)
    barrier = pltpu.get_barrier_semaphore()

    def greet(peer, mine, theirs):
        pl.semaphore_signal(barrier, inc=1, device_id={"table": peer}, device_id_type=pl.DeviceIdType.MESH)

    in_range(z_count, me, 0, z_count // 2, greet)
    for peer in near:
        pl.semaphore_signal(barrier, inc=1, device_id={"bal": peer}, device_id_type=pl.DeviceIdType.MESH)

    tokens = ids_ref.shape[1]
    per = tokens // n
    shard = cold_ref.shape[0]
    hot_count = hot_ref.shape[0]
    loads[6].wait()
    ids_row = jnp.broadcast_to(ids_ref[...].astype(F32), (tokens, tokens))
    diag = iota((tokens, tokens), 0) == iota((tokens, tokens), 1)
    ids = jnp.sum(jnp.where(diag, ids_row, 0.0), axis=1, keepdims=True).astype(jnp.int32)
    lines = slot_ref.shape[0]
    pick = one_hot(iota((tokens, lines), 1) == ids // 128)
    loads[0].wait()
    slots = slot_ref[...]
    high = dot(pick, (slots // 8).astype(F32).astype(BF))
    low = dot(pick, (slots % 8).astype(F32).astype(BF))
    lane = iota((tokens, 128), 1)
    hot_index = jnp.sum(jnp.where(lane == ids % 128, high * 8.0 + low, 0.0), axis=1, keepdims=True).astype(jnp.int32)
    owner = ids // shard
    row = ids % shard
    away = (owner // 2 - z + z_count) % z_count
    rank = jnp.where(away == 0, 0, jnp.where(away <= z_count // 2, 2 * away - 1, 2 * (z_count - away)))
    owner = rank * 2 + owner % 2
    cold = hot_index >= hot_count
    marks = one_hot((lane == owner) & cold)
    before = dot(one_hot(iota((tokens, tokens), 1) < iota((tokens, tokens), 0)), marks)
    place = jnp.sum(before * marks.astype(F32), axis=1, keepdims=True).astype(jnp.int32)
    digits = jnp.where(
        lane == place, (row // 8).astype(F32), jnp.where(lane == place + per, (row % 8).astype(F32), 0.0)
    ).astype(BF)
    ask[...] = dot(marks, digits, 0, 0)[:n].reshape(n, 1, 128)

    pl.semaphore_wait(barrier, n - 1 + len(near))

    def send(src, dst, low, high, out_sem, in_sem):
        def one(peer, mine, theirs):
            pltpu.make_async_remote_copy(
                src_ref=src.at[mine], dst_ref=dst.at[theirs], send_sem=out_sem, recv_sem=in_sem,
                device_id={"table": peer}, device_id_type=pl.DeviceIdType.MESH,
            ).start()

        in_range(z_count, me, low, high, one)

    def settle(ref, first, last, sem):
        part = ref.at[pl.ds(first, last - first)]
        pltpu.make_async_copy(part, part, sem).wait()

    for k, (low_d, high_d, _, _) in reversed(list(enumerate(batches))):
        send(ask, asked, low_d, high_d, ask_send, ask_recv.at[k])
    asked[core] = ask[core]
    loads[2].wait()
    emb_ref[...] = dot(one_hot(iota((tokens, hot_count), 1) == hot_index), hot_ref[...])
    loads[1].wait()

    pieces = cold_ref.shape[1] // 128
    for k, (low_d, high_d, first, last) in enumerate(batches):
        settle(asked, first + (k == 0), last, ask_recv.at[k])
        count = (last - first) * per
        spread = one_hot(iota((count, last - first), 0) // per == iota((count, last - first), 1))
        got = dot(spread, asked[first:last].reshape(last - first, 128).astype(BF))
        lanes = iota((count, 128), 1)
        turn = iota((count, 128), 0) % per
        want = jnp.sum(
            jnp.where(lanes == turn, got * 8.0, jnp.where(lanes == turn + per, got, 0.0)), axis=1, keepdims=True
        ).astype(jnp.int32)
        rows = dot(one_hot(iota((count, shard), 1) == want), cold_ref[...])
        base = first * per * pieces
        for j in range(pieces):
            wide[pl.ds(base + j, count, stride=pieces), :] = rows[:, j * 128 : (j + 1) * 128]
        found[first:last] = (
            wide[base : base + count * pieces].astype(BF).reshape(last - first, per * pieces, 128)
        )
        send(found, reply, low_d, high_d, reply_send, reply_recv)
        if k == 0:
            reply[core] = found[core]
    take = one_hot(iota((tokens, tokens), 1) == jnp.where(cold, owner * per + place, -1))
    meanwhile()
    settle(reply, 1, n, reply_recv)

    wide[...] = reply[...].reshape(wide.shape).astype(F32)
    for j in range(pieces):
        cut = slice(j * 128, (j + 1) * 128)
        piece = wide[pl.ds(j, tokens, stride=pieces), :].astype(BF)
        emb_ref[:, cut] += dot(take, piece)

    def end():
        settle(ask, 1, n, ask_send)
        settle(found, 1, n, reply_send)

    return end


def normalised(values):
    mean = jnp.mean(values, axis=-1, keepdims=True)
    centred = values - mean
    scale = lax.rsqrt(jnp.mean(centred * centred, axis=-1, keepdims=True) + 1e-05)
    return centred * scale, scale


def silu_both(v):
    sig = 0.5 * jnp.tanh(0.5 * v) + 0.5
    act = v * sig
    return act, sig + act * (1.0 - sig)


CHUNKS = 5
WIDE = 256


class Ring:
    def __init__(self, g, in1, out1, total, tot_bf, in2, out2, send1, recv1, send2, recv2):
        self.g, self.in1, self.out1, self.total, self.tot_bf = g, in1, out1, total, tot_bf
        self.in2, self.out2 = in2, out2
        self.sems = ((send1, recv1), (send2, recv2))
        me = lax.axis_index("bal")
        x, y = me // 4, me % 4
        self.places = ((x, y), (y, x))
        along_x = tuple((x + step) % 4 * 4 + y for step in (1, 3))
        along_y = tuple(x * 4 + (y + step) % 4 for step in (1, 3))
        self.peers = ((along_x, along_y), (along_y, along_x))
        self.near = (*along_x, *along_y)
        self.sent = {}

    def post(self, stage, c, half, way, msg):
        at = self.places[half][stage]
        step = (1, 3)[way]
        if stage == 0:
            mine, other = pl.ds(2 * way, 2), pl.ds(2 - 2 * way, 2)
            src, land, out = self.g, self.in1, self.out1
        else:
            mid = self.tot_bf.shape[3] // 2
            mine, other = pl.ds(mid * way, mid), pl.ds(mid - mid * way, mid)
            src, land, out = self.tot_bf, self.in2, self.out2
        ref = (
            src.at[c, half, (at + 2) % 4, mine],
            src.at[c, half, (at + step) % 4, other],
            out.at[c, half, way],
        )[msg]
        send, recv = self.sems[stage]
        copy = pltpu.make_async_remote_copy(
            src_ref=ref, dst_ref=land.at[c, half, way, msg],
            send_sem=send.at[c, half, way, msg], recv_sem=recv.at[c, half, way, msg],
            device_id={"bal": self.peers[half][stage][way]}, device_id_type=pl.DeviceIdType.MESH,
        )
        copy.start()
        self.sent[stage, c, half, way, msg] = copy

    def arrive(self, stage, c, half, way, msg):
        self.sent[stage, c, half, way, msg].wait_recv()

    def start(self, stage, c):
        for msg in (0, 1):
            for half in range(2):
                for way in range(2):
                    self.post(stage, c, half, way, msg)

    def relay(self, stage, c):
        for half in range(2):
            at = self.places[half][stage]
            for way in range(2):
                self.arrive(stage, c, half, way, 0)
                to = (at + (1, 3)[way]) % 4
                if stage == 0:
                    own = self.g[c, half, to, pl.ds(2 * way, 2)].astype(F32)
                    self.out1[c, half, way] = (own + self.in1[c, half, way, 0].astype(F32)).astype(BF)
                else:
                    mid = self.tot_bf.shape[3] // 2
                    own = self.total[c, half, to, pl.ds(mid * way, mid)]
                    self.out2[c, half, way] = (own + self.in2[c, half, way, 0].astype(F32)).astype(BF)
                self.post(stage, c, half, way, 2)

    def turn(self, c):
        for half in range(2):
            a = self.places[half][0]
            for way in range(2):
                self.arrive(0, c, half, way, 1)
                self.arrive(0, c, half, way, 2)
            for part in range(2):
                here = pl.ds(2 * part, 2)
                t = (
                    self.g[c, half, a, here].astype(F32)
                    + self.in1[c, half, part, 2].astype(F32)
                    + self.in1[c, half, 1 - part, 1].astype(F32)
                )
                self.total[c, half, here] = t
                self.tot_bf[c, half, here] = t.astype(BF)
        self.start(1, c)

    def finish(self, c, store):
        mid = self.tot_bf.shape[3] // 2
        for half in range(2):
            b = self.places[half][1]
            for way in range(2):
                self.arrive(1, c, half, way, 1)
                self.arrive(1, c, half, way, 2)
            for part in range(2):
                rows = pl.ds(mid * part, mid)
                store(
                    c, half, rows,
                    self.total[c, half, b, rows]
                    + self.in2[c, half, part, 2].astype(F32)
                    + self.in2[c, half, 1 - part, 1].astype(F32),
                )

    def drain(self):
        for copy in self.sent.values():
            copy.wait_send()


def layer_kernel(
    n_table, grad_scale, ids_hbm, len_hbm, slot_hbm, hot_hbm, cold_hbm, cot_hbm, wu_hbm, wo_hbm,
    out_ref, first_ref, second_ref,
    ids_ref, len_ref, slot_ref, hot_ref, cold_ref, cot_ref, wu_ref, wo_ref, ask, asked, wide, found, reply, emb_ref,
    slope, acts, attn, attn_slope, mixed, grads, signal_ref, back_ref,
    load_sem, ask_send, ask_recv, reply_send, reply_recv, *ring_refs,
):
    tokens, features = emb_ref.shape
    loads = [
        pltpu.make_async_copy(src, dst, load_sem.at[k])
        for k, (src, dst) in enumerate((
            (slot_hbm, slot_ref), (cold_hbm, cold_ref), (hot_hbm, hot_ref),
            (cot_hbm, cot_ref), (wo_hbm, wo_ref), (wu_hbm, wu_ref), (ids_hbm, ids_ref), (len_hbm, len_ref),
        ))
    ]
    for k in (6, 7, 0, 1, 2, 3, 4, 5):
        loads[k].start()
    ring = Ring(*ring_refs)
    users = tokens // MAXLEN
    head = features // HEADS
    first = (lax.axis_index("table") * lax.axis_size("bal") + lax.axis_index("bal")) * users

    def valid_below():
        return [len_ref[first + u] for u in range(users)]

    def cotangent():
        for load in loads[3:6] + loads[7:]:
            load.wait()
        lengths = valid_below()
        at = iota((tokens, 1), 0)
        ends = jnp.full((tokens, 1), lengths[0], jnp.int32)
        for u in range(1, users):
            ends = jnp.where(at >= u * MAXLEN, u * MAXLEN + lengths[u], ends)
        signal = (jnp.where(at < ends, cot_ref[...].astype(F32), 0.0) * grad_scale).astype(BF)
        signal_ref[...] = signal
        back_ref[...] = dot(signal, wo_ref[...], 1, 1).astype(BF)

    end = lookup(
        n_table, loads, ring.near, cotangent, ids_ref, slot_ref, hot_ref, cold_ref, ask, asked, wide, found, reply,
        emb_ref, ask_send, ask_recv, reply_send, reply_recv,
    )
    emb = emb_ref[...]
    normed = normalised(emb)[0].astype(BF)
    for b in (2, 3, 1, 0):
        cut = slice(b * features, (b + 1) * features)
        act, dact = silu_both(dot(normed, wu_ref[:, cut]))
        acts[:, cut] = act.astype(BF)
        slope[:, cut] = dact
    lengths = valid_below()
    i, j = iota((MAXLEN, MAXLEN), 0), iota((MAXLEN, MAXLEN), 1)
    scale = 1.0 / math.sqrt(head)

    def part(b, u, h):
        at = b * features + h * head
        return acts[u * MAXLEN : (u + 1) * MAXLEN, at : at + head]

    for u in range(users):
        allowed = (j <= i) & (i < lengths[u])
        for h in range(HEADS):
            s = dot(part(2, u, h), part(3, u, h), 1, 1) * scale
            act, dact = silu_both(s)
            w = jnp.where(allowed, act, 0.0).astype(BF)
            attn[u * HEADS + h] = w
            attn_slope[u * HEADS + h] = jnp.where(allowed, dact * scale, 0.0)
            mixed[u * MAXLEN : (u + 1) * MAXLEN, h * head : (h + 1) * head] = dot(w, part(1, u, h))

    n, rstd = normalised(mixed[...])
    gate = acts[:, :features].astype(F32)
    gated = (n * gate).astype(BF)
    signal = signal_ref[...]

    def spread(c, left, right):
        for half in range(2):
            value = dot(left, right[:, half * WIDE : (half + 1) * WIDE], 0, 0).astype(BF)
            height = features // 16
            for b in range(16):
                x, y = divmod(b, 4)
                f, s = (x, y) if half == 0 else (y, x)
                ring.g[c, half, f, s] = value[b * height : (b + 1) * height]
        ring.start(0, c)

    spread(0, gated, signal)
    back = back_ref[...].astype(F32)
    grads[:, :features] = ((back * n).astype(BF).astype(F32) * slope[:, :features]).astype(BF)
    spread(1, normed, grads[:, :features])
    dn = back * gate
    mixed[...] = rstd * (
        dn - jnp.mean(dn, axis=-1, keepdims=True) - n * jnp.mean(dn * n, axis=-1, keepdims=True)
    )
    for u in range(users):
        rows = slice(u * MAXLEN, (u + 1) * MAXLEN)
        for h in range(HEADS):
            dm = mixed[rows, h * head : (h + 1) * head].astype(BF)
            w = attn[u * HEADS + h]
            dw = dot(dm, part(1, u, h), 1, 1).astype(BF).astype(F32)
            ds = (dw * attn_slope[u * HEADS + h]).astype(BF)
            for b, d in (
                (1, dot(w, dm, 0, 0)),
                (2, dot(ds, part(3, u, h))),
                (3, dot(ds, part(2, u, h), 0, 0)),
            ):
                cols = slice(b * features + h * head, b * features + (h + 1) * head)
                grads[rows, cols] = (d.astype(BF).astype(F32) * slope[rows, cols]).astype(BF)
    ring.relay(0, 0)
    spread(2, normed, grads[:, features : 2 * features])
    ring.relay(0, 1)
    spread(3, normed, grads[:, 2 * features : 3 * features])
    spread(4, normed, grads[:, 3 * features :])
    ring.relay(0, 2)
    ring.turn(0)
    ring.relay(0, 3)
    ring.turn(1)
    out_ref[...] = (emb + dot(gated, wo_ref[...])).astype(BF)
    ring.relay(0, 4)
    ring.relay(1, 0)
    ring.turn(2)
    ring.relay(1, 1)
    ring.turn(3)

    def store(c, half, rows, value):
        if c == 0:
            second_ref[rows, half * WIDE : (half + 1) * WIDE] = value
        else:
            low = (c - 1) * features + half * WIDE
            first_ref[rows, low : low + WIDE] = value

    ring.relay(1, 2)
    ring.finish(0, store)
    ring.turn(4)
    ring.relay(1, 3)
    ring.finish(1, store)
    ring.finish(2, store)
    ring.relay(1, 4)
    ring.finish(3, store)
    ring.finish(4, store)
    ring.drain()
    end()


def ring_scratch(height):
    dma = pltpu.SemaphoreType.DMA((CHUNKS, 2, 2, 3))
    return [
        pltpu.VMEM((CHUNKS, 2, 4, 4, height, WIDE), BF),
        pltpu.VMEM((CHUNKS, 2, 2, 3, 2, height, WIDE), BF),
        pltpu.VMEM((CHUNKS, 2, 2, 2, height, WIDE), BF),
        pltpu.VMEM((CHUNKS, 2, 4, height, WIDE), F32),
        pltpu.VMEM((CHUNKS, 2, 4, height, WIDE), BF),
        pltpu.VMEM((CHUNKS, 2, 2, 3, height // 2, WIDE), BF),
        pltpu.VMEM((CHUNKS, 2, 2, height // 2, WIDE), BF),
        dma, dma, dma, dma,
    ]


def layer(n, grad_scale, ids, hot_slot, hot_rows, cold_rows, lengths, cot, wu, wo):
    tokens, features = cot.shape
    users = tokens // MAXLEN
    height = features // 16
    piece = features // 128 * (tokens // n)
    lines = hot_slot.reshape(-1, 128)
    return pl.pallas_call(
        functools.partial(layer_kernel, n, grad_scale),
        out_shape=(
            jax.ShapeDtypeStruct((tokens, features), BF),
            jax.ShapeDtypeStruct((height, 4 * features), F32),
            jax.ShapeDtypeStruct((height, features), F32),
        ),
        in_specs=[HBM] * 8,
        out_specs=(VMEM, VMEM, VMEM),
        scratch_shapes=[
            pltpu.VMEM((1, tokens), jnp.int32),
            pltpu.SMEM(lengths.shape, jnp.int32),
            pltpu.VMEM(lines.shape, jnp.int32),
            pltpu.VMEM(hot_rows.shape, BF),
            pltpu.VMEM(cold_rows.shape, BF),
            pltpu.VMEM(cot.shape, BF),
            pltpu.VMEM(wu.shape, BF),
            pltpu.VMEM(wo.shape, BF),
            pltpu.VMEM((n, 1, 128), F32),
            pltpu.VMEM((n, 1, 128), F32),
            pltpu.VMEM((n * piece, 128), F32),
            pltpu.VMEM((n, piece, 128), BF),
            pltpu.VMEM((n, piece, 128), BF),
            pltpu.VMEM((tokens, features), F32),
            pltpu.VMEM((tokens, 4 * features), F32),
            pltpu.VMEM((tokens, 4 * features), BF),
            pltpu.VMEM((users * HEADS, MAXLEN, MAXLEN), BF),
            pltpu.VMEM((users * HEADS, MAXLEN, MAXLEN), F32),
            pltpu.VMEM((tokens, features), F32),
            pltpu.VMEM((tokens, 4 * features), BF),
            pltpu.VMEM((tokens, features), BF),
            pltpu.VMEM((tokens, features), BF),
            pltpu.SemaphoreType.DMA((8,)),
            pltpu.SemaphoreType.DMA,
            pltpu.SemaphoreType.DMA((4,)),
            pltpu.SemaphoreType.DMA,
            pltpu.SemaphoreType.DMA,
            *ring_scratch(height),
        ],
        compiler_params=pltpu.CompilerParams(
            collective_id=0, has_side_effects=True, vmem_limit_bytes=36 * 2**20
        ),
        name="layer",
    )(
        *(
            pltpu.with_memory_space_constraint(a, pltpu.HBM)
            for a in (ids.reshape(1, tokens), lengths, lines, hot_rows, cold_rows, cot, wu, wo)
        ),
    )


def per_device(item_ids, hot_slot, hot_rows, cold_rows, hist_lengths, out_grad, w_uvqk, w_out):
    grad_scale = 1.0 / math.sqrt(lax.axis_size("bal") * out_grad.shape[0])
    return layer(
        lax.axis_size("table"), grad_scale, item_ids, hot_slot, hot_rows, cold_rows, hist_lengths, out_grad, w_uvqk, w_out
    )


def solution(mesh):
    both = P(("table", "bal"), None)
    return jax.shard_map(
        per_device,
        mesh=mesh,
        in_specs=(P(("table", "bal")), P(), P(), P("table", None), P(), both, P(), P()),
        out_specs=(both, both, both),
        check_vma=False,
    )
```

```python
import functools
import math

import jax
import jax.numpy as jnp
from jax import lax
from jax.experimental import pallas as pl
from jax.experimental.pallas import tpu as pltpu
from jax.sharding import PartitionSpec as P

HEADS = 4
MAXLEN = 128
BF, F32 = jnp.bfloat16, jnp.float32
VMEM = pl.BlockSpec(memory_space=pltpu.VMEM)
HBM = pl.BlockSpec(memory_space=pltpu.HBM)


def dot(a, b, ca=1, cb=0):
    return lax.dot_general(a, b, (((ca,), (cb,)), ((), ())), preferred_element_type=F32)


def iota(shape, dim):
    return lax.broadcasted_iota(jnp.int32, shape, dim)


def one_hot(cond):
    return jnp.where(cond, 1.0, 0.0).astype(BF)


def at_distance(z_count, me, d, do):
    z, core = me // 2, me % 2
    for step, rank, mirrored in ((d, 2 * d - 1, 2 * d), (z_count - d, 2 * d, 2 * d - 1)):
        for c in range(2):
            do(lax.rem(z + step, z_count) * 2 + c, rank * 2 + c, mirrored * 2 + core)


def in_range(z_count, me, low, high, do):
    z, core = me // 2, me % 2
    if high == z_count // 2:
        for c in range(2):
            do(lax.rem(z + high, z_count) * 2 + c, (z_count - 1) * 2 + c, (z_count - 1) * 2 + core)
        high -= 1
    least = max(low, 1)

    def one(i, _):
        at_distance(z_count, me, high - i, do)
        return 0

    lax.fori_loop(0, high - least + 1, one, 0)
    if low == 0:
        do(z * 2 + 1 - core, 1 - core, core)


def ranges(z_count):
    ends = [z_count // 8 - 1, z_count // 4 - 1, 3 * z_count // 8 - 1, z_count // 2]
    low, first, out = 0, 0, []
    for high in ends:
        last = 2 * z_count if high == z_count // 2 else 4 * high + 2
        out.append((low, high, first, last))
        low, first = high + 1, last
    return out


def lookup(
    n, loads, near, meanwhile, ids_ref, slot_ref, hot_ref, cold_ref, ask, asked, wide, found, reply, emb_ref,
    ask_send, ask_recv, reply_send, reply_recv,
):
    z_count = n // 2
    me = lax.axis_index("table")
    z, core = me // 2, me % 2
    batches = ranges(z_count)
    barrier = pltpu.get_barrier_semaphore()

    def greet(peer, mine, theirs):
        pl.semaphore_signal(barrier, inc=1, device_id={"table": peer}, device_id_type=pl.DeviceIdType.MESH)

    in_range(z_count, me, 0, z_count // 2, greet)
    for peer in near:
        pl.semaphore_signal(barrier, inc=1, device_id={"bal": peer}, device_id_type=pl.DeviceIdType.MESH)

    tokens = ids_ref.shape[1]
    per = tokens // n
    shard = cold_ref.shape[0]
    hot_count = hot_ref.shape[0]
    loads[6].wait()
    ids_row = jnp.broadcast_to(ids_ref[...].astype(F32), (tokens, tokens))
    diag = iota((tokens, tokens), 0) == iota((tokens, tokens), 1)
    ids = jnp.sum(jnp.where(diag, ids_row, 0.0), axis=1, keepdims=True).astype(jnp.int32)
    lines = slot_ref.shape[0]
    pick = one_hot(iota((tokens, lines), 1) == ids // 128)
    loads[0].wait()
    slots = slot_ref[...]
    high = dot(pick, (slots // 8).astype(F32).astype(BF))
    low = dot(pick, (slots % 8).astype(F32).astype(BF))
    lane = iota((tokens, 128), 1)
    hot_index = jnp.sum(jnp.where(lane == ids % 128, high * 8.0 + low, 0.0), axis=1, keepdims=True).astype(jnp.int32)
    owner = ids // shard
    row = ids % shard
    away = (owner // 2 - z + z_count) % z_count
    rank = jnp.where(away == 0, 0, jnp.where(away <= z_count // 2, 2 * away - 1, 2 * (z_count - away)))
    owner = rank * 2 + owner % 2
    cold = hot_index >= hot_count
    marks = one_hot((lane == owner) & cold)
    before = dot(one_hot(iota((tokens, tokens), 1) < iota((tokens, tokens), 0)), marks)
    place = jnp.sum(before * marks.astype(F32), axis=1, keepdims=True).astype(jnp.int32)
    digits = jnp.where(
        lane == place, (row // 8).astype(F32), jnp.where(lane == place + per, (row % 8).astype(F32), 0.0)
    ).astype(BF)
    ask[...] = dot(marks, digits, 0, 0)[:n].reshape(n, 1, 128)

    pl.semaphore_wait(barrier, n - 1 + len(near))

    def send(src, dst, low, high, out_sem, in_sem):
        def one(peer, mine, theirs):
            pltpu.make_async_remote_copy(
                src_ref=src.at[mine], dst_ref=dst.at[theirs], send_sem=out_sem, recv_sem=in_sem,
                device_id={"table": peer}, device_id_type=pl.DeviceIdType.MESH,
            ).start()

        in_range(z_count, me, low, high, one)

    def settle(ref, first, last, sem):
        part = ref.at[pl.ds(first, last - first)]
        pltpu.make_async_copy(part, part, sem).wait()

    for k, (low_d, high_d, _, _) in reversed(list(enumerate(batches))):
        send(ask, asked, low_d, high_d, ask_send, ask_recv.at[k])
    asked[core] = ask[core]
    loads[2].wait()
    emb_ref[...] = dot(one_hot(iota((tokens, hot_count), 1) == hot_index), hot_ref[...])
    loads[1].wait()

    pieces = cold_ref.shape[1] // 128
    for k, (low_d, high_d, first, last) in enumerate(batches):
        settle(asked, first + (k == 0), last, ask_recv.at[k])
        count = (last - first) * per
        spread = one_hot(iota((count, last - first), 0) // per == iota((count, last - first), 1))
        got = dot(spread, asked[first:last].reshape(last - first, 128).astype(BF))
        lanes = iota((count, 128), 1)
        turn = iota((count, 128), 0) % per
        want = jnp.sum(
            jnp.where(lanes == turn, got * 8.0, jnp.where(lanes == turn + per, got, 0.0)), axis=1, keepdims=True
        ).astype(jnp.int32)
        rows = dot(one_hot(iota((count, shard), 1) == want), cold_ref[...])
        base = first * per * pieces
        for j in range(pieces):
            wide[pl.ds(base + j, count, stride=pieces), :] = rows[:, j * 128 : (j + 1) * 128]
        found[first:last] = (
            wide[base : base + count * pieces].astype(BF).reshape(last - first, per * pieces, 128)
        )
        send(found, reply, low_d, high_d, reply_send, reply_recv)
        if k == 0:
            reply[core] = found[core]
    take = one_hot(iota((tokens, tokens), 1) == jnp.where(cold, owner * per + place, -1))
    meanwhile()
    settle(reply, 1, n, reply_recv)

    wide[...] = reply[...].reshape(wide.shape).astype(F32)
    for j in range(pieces):
        cut = slice(j * 128, (j + 1) * 128)
        piece = wide[pl.ds(j, tokens, stride=pieces), :].astype(BF)
        emb_ref[:, cut] += dot(take, piece)

    def end():
        settle(ask, 1, n, ask_send)
        settle(found, 1, n, reply_send)

    return end


def normalised(values):
    mean = jnp.mean(values, axis=-1, keepdims=True)
    centred = values - mean
    scale = lax.rsqrt(jnp.mean(centred * centred, axis=-1, keepdims=True) + 1e-05)
    return centred * scale, scale


def silu_both(v):
    sig = 0.5 * jnp.tanh(0.5 * v) + 0.5
    act = v * sig
    return act, sig + act * (1.0 - sig)


WIDE = 256
GROUPS = ((4, 0), (1, 2, 3))


class Ring:
    def __init__(self, send1, recv1, send2, recv2, *refs):
        count = len(GROUPS)
        self.g, self.in1, self.out1, self.total, self.tot_bf, self.in2, self.out2 = (
            refs[k * count : (k + 1) * count] for k in range(7)
        )
        self.sems = ((send1, recv1), (send2, recv2))
        me = lax.axis_index("bal")
        x, y = me // 4, me % 4
        self.places = ((x, y), (y, x))
        along_x = tuple((x + step) % 4 * 4 + y for step in (1, 3))
        along_y = tuple(x * 4 + (y + step) % 4 for step in (1, 3))
        self.peers = ((along_x, along_y), (along_y, along_x))
        self.near = (*along_x, *along_y)
        self.sent = {}

    def post(self, stage, c, half, way, msg):
        at = self.places[half][stage]
        step = (1, 3)[way]
        if stage == 0:
            mine, other = pl.ds(2 * way, 2), pl.ds(2 - 2 * way, 2)
            src, land, out = self.g, self.in1, self.out1
        else:
            mid = self.tot_bf[c].shape[2] // 2
            mine, other = pl.ds(mid * way, mid), pl.ds(mid - mid * way, mid)
            src, land, out = self.tot_bf, self.in2, self.out2
        ref = (
            src[c].at[half, (at + 2) % 4, mine],
            src[c].at[half, (at + step) % 4, other],
            out[c].at[half, way],
        )[msg]
        send, recv = self.sems[stage]
        copy = pltpu.make_async_remote_copy(
            src_ref=ref, dst_ref=land[c].at[half, way, msg],
            send_sem=send.at[c, half, way, msg], recv_sem=recv.at[c, half, way, msg],
            device_id={"bal": self.peers[half][stage][way]}, device_id_type=pl.DeviceIdType.MESH,
        )
        copy.start()
        self.sent[stage, c, half, way, msg] = copy

    def arrive(self, stage, c, half, way, msg):
        self.sent[stage, c, half, way, msg].wait_recv()

    def start(self, stage, c):
        for msg in (0, 1):
            for half in range(2):
                for way in range(2):
                    self.post(stage, c, half, way, msg)

    def relay(self, stage, c):
        for half in range(2):
            at = self.places[half][stage]
            for way in range(2):
                self.arrive(stage, c, half, way, 0)
                to = (at + (1, 3)[way]) % 4
                if stage == 0:
                    own = self.g[c][half, to, pl.ds(2 * way, 2)].astype(F32)
                    self.out1[c][half, way] = (own + self.in1[c][half, way, 0].astype(F32)).astype(BF)
                else:
                    mid = self.tot_bf[c].shape[2] // 2
                    own = self.total[c][half, to, pl.ds(mid * way, mid)]
                    self.out2[c][half, way] = (own + self.in2[c][half, way, 0].astype(F32)).astype(BF)
                self.post(stage, c, half, way, 2)

    def turn(self, c):
        for half in range(2):
            a = self.places[half][0]
            for way in range(2):
                self.arrive(0, c, half, way, 1)
                self.arrive(0, c, half, way, 2)
            for part in range(2):
                here = pl.ds(2 * part, 2)
                t = (
                    self.g[c][half, a, here].astype(F32)
                    + self.in1[c][half, part, 2].astype(F32)
                    + self.in1[c][half, 1 - part, 1].astype(F32)
                )
                self.total[c][half, here] = t
                self.tot_bf[c][half, here] = t.astype(BF)
        self.start(1, c)

    def finish(self, c, store):
        mid = self.tot_bf[c].shape[2] // 2
        for half in range(2):
            b = self.places[half][1]
            for way in range(2):
                self.arrive(1, c, half, way, 1)
                self.arrive(1, c, half, way, 2)
            for part in range(2):
                rows = pl.ds(mid * part, mid)
                store(
                    c, half, rows,
                    self.total[c][half, b, rows]
                    + self.in2[c][half, part, 2].astype(F32)
                    + self.in2[c][half, 1 - part, 1].astype(F32),
                )

    def drain(self):
        for copy in self.sent.values():
            copy.wait_send()


def layer_kernel(
    n_table, grad_scale, ids_hbm, len_hbm, slot_hbm, hot_hbm, cold_hbm, cot_hbm, wu_hbm, wo_hbm,
    out_ref, first_ref, second_ref,
    ids_ref, len_ref, slot_ref, hot_ref, cold_ref, cot_ref, wu_ref, wo_ref, ask, asked, wide, found, reply, emb_ref,
    slope, acts, attn, attn_slope, mixed, grads, signal_ref, back_ref,
    load_sem, ask_send, ask_recv, reply_send, reply_recv, *ring_refs,
):
    tokens, features = emb_ref.shape
    loads = [
        pltpu.make_async_copy(src, dst, load_sem.at[k])
        for k, (src, dst) in enumerate((
            (slot_hbm, slot_ref), (cold_hbm, cold_ref), (hot_hbm, hot_ref),
            (cot_hbm, cot_ref), (wo_hbm, wo_ref), (wu_hbm, wu_ref), (ids_hbm, ids_ref), (len_hbm, len_ref),
        ))
    ]
    for k in (6, 7, 0, 1, 2, 3, 4, 5):
        loads[k].start()
    ring = Ring(*ring_refs)
    users = tokens // MAXLEN
    head = features // HEADS
    first = (lax.axis_index("table") * lax.axis_size("bal") + lax.axis_index("bal")) * users

    def valid_below():
        return [len_ref[first + u] for u in range(users)]

    def cotangent():
        for load in loads[3:6] + loads[7:]:
            load.wait()
        lengths = valid_below()
        at = iota((tokens, 1), 0)
        ends = jnp.full((tokens, 1), lengths[0], jnp.int32)
        for u in range(1, users):
            ends = jnp.where(at >= u * MAXLEN, u * MAXLEN + lengths[u], ends)
        signal = (jnp.where(at < ends, cot_ref[...].astype(F32), 0.0) * grad_scale).astype(BF)
        signal_ref[...] = signal
        back_ref[...] = dot(signal, wo_ref[...], 1, 1).astype(BF)

    end = lookup(
        n_table, loads, ring.near, cotangent, ids_ref, slot_ref, hot_ref, cold_ref, ask, asked, wide, found, reply,
        emb_ref, ask_send, ask_recv, reply_send, reply_recv,
    )
    emb = emb_ref[...]
    normed = normalised(emb)[0].astype(BF)
    for b in (2, 3, 1, 0):
        cut = slice(b * features, (b + 1) * features)
        act, dact = silu_both(dot(normed, wu_ref[:, cut]))
        acts[:, cut] = act.astype(BF)
        slope[:, cut] = dact
    lengths = valid_below()
    i, j = iota((MAXLEN, MAXLEN), 0), iota((MAXLEN, MAXLEN), 1)
    scale = 1.0 / math.sqrt(head)

    def part(b, u, h):
        at = b * features + h * head
        return acts[u * MAXLEN : (u + 1) * MAXLEN, at : at + head]

    for u in range(users):
        allowed = (j <= i) & (i < lengths[u])
        for h in range(HEADS):
            s = dot(part(2, u, h), part(3, u, h), 1, 1) * scale
            act, dact = silu_both(s)
            w = jnp.where(allowed, act, 0.0).astype(BF)
            attn[u * HEADS + h] = w
            attn_slope[u * HEADS + h] = jnp.where(allowed, dact * scale, 0.0)
            mixed[u * MAXLEN : (u + 1) * MAXLEN, h * head : (h + 1) * head] = dot(w, part(1, u, h))

    n, rstd = normalised(mixed[...])
    gate = acts[:, :features].astype(F32)
    gated = (n * gate).astype(BF)
    signal = signal_ref[...]

    def spread(block, left, right):
        [c] = [c for c, group in enumerate(GROUPS) if block in group]
        at = GROUPS[c].index(block) * WIDE
        height = features // 16
        for half in range(2):
            value = dot(left, right[:, half * WIDE : (half + 1) * WIDE], 0, 0).astype(BF)
            for b in range(16):
                x, y = divmod(b, 4)
                f, s = (x, y) if half == 0 else (y, x)
                ring.g[c][half, f, s, :, at : at + WIDE] = value[b * height : (b + 1) * height]
        if block == GROUPS[c][-1]:
            ring.start(0, c)

    spread(4, gated, signal)
    back = back_ref[...].astype(F32)
    grads[:, :features] = ((back * n).astype(BF).astype(F32) * slope[:, :features]).astype(BF)
    spread(0, normed, grads[:, :features])
    dn = back * gate
    mixed[...] = rstd * (
        dn - jnp.mean(dn, axis=-1, keepdims=True) - n * jnp.mean(dn * n, axis=-1, keepdims=True)
    )
    for u in range(users):
        rows = slice(u * MAXLEN, (u + 1) * MAXLEN)
        for h in range(HEADS):
            dm = mixed[rows, h * head : (h + 1) * head].astype(BF)
            w = attn[u * HEADS + h]
            dw = dot(dm, part(1, u, h), 1, 1).astype(BF).astype(F32)
            ds = (dw * attn_slope[u * HEADS + h]).astype(BF)
            for b, d in (
                (1, dot(w, dm, 0, 0)),
                (2, dot(ds, part(3, u, h))),
                (3, dot(ds, part(2, u, h), 0, 0)),
            ):
                cols = slice(b * features + h * head, b * features + (h + 1) * head)
                grads[rows, cols] = (d.astype(BF).astype(F32) * slope[rows, cols]).astype(BF)
    for b in range(1, 4):
        spread(b, normed, grads[:, b * features : (b + 1) * features])

    def store(c, half, rows, value):
        for k, block in enumerate(GROUPS[c]):
            piece = value[:, k * WIDE : (k + 1) * WIDE]
            low = half * WIDE
            if block == 4:
                second_ref[rows, low : low + WIDE] = piece
            else:
                first_ref[rows, block * features + low : block * features + low + WIDE] = piece

    chunks = range(len(GROUPS))
    for c in chunks:
        ring.relay(0, c)
    out_ref[...] = (emb + dot(gated, wo_ref[...])).astype(BF)
    for c in chunks:
        ring.turn(c)
    for c in chunks:
        ring.relay(1, c)
    for c in chunks:
        ring.finish(c, store)
    ring.drain()
    end()


def ring_scratch(height):
    dma = pltpu.SemaphoreType.DMA((len(GROUPS), 2, 2, 3))
    shapes = (
        ((2, 4, 4, height), BF),
        ((2, 2, 3, 2, height), BF),
        ((2, 2, 2, height), BF),
        ((2, 4, height), F32),
        ((2, 4, height), BF),
        ((2, 2, 3, height // 2), BF),
        ((2, 2, height // 2), BF),
    )
    return [dma] * 4 + [
        pltpu.VMEM((*shape, WIDE * len(group)), kind) for shape, kind in shapes for group in GROUPS
    ]


def layer(n, grad_scale, ids, hot_slot, hot_rows, cold_rows, lengths, cot, wu, wo):
    tokens, features = cot.shape
    users = tokens // MAXLEN
    height = features // 16
    piece = features // 128 * (tokens // n)
    lines = hot_slot.reshape(-1, 128)
    return pl.pallas_call(
        functools.partial(layer_kernel, n, grad_scale),
        out_shape=(
            jax.ShapeDtypeStruct((tokens, features), BF),
            jax.ShapeDtypeStruct((height, 4 * features), F32),
            jax.ShapeDtypeStruct((height, features), F32),
        ),
        in_specs=[HBM] * 8,
        out_specs=(VMEM, VMEM, VMEM),
        scratch_shapes=[
            pltpu.VMEM((1, tokens), jnp.int32),
            pltpu.SMEM(lengths.shape, jnp.int32),
            pltpu.VMEM(lines.shape, jnp.int32),
            pltpu.VMEM(hot_rows.shape, BF),
            pltpu.VMEM(cold_rows.shape, BF),
            pltpu.VMEM(cot.shape, BF),
            pltpu.VMEM(wu.shape, BF),
            pltpu.VMEM(wo.shape, BF),
            pltpu.VMEM((n, 1, 128), F32),
            pltpu.VMEM((n, 1, 128), F32),
            pltpu.VMEM((n * piece, 128), F32),
            pltpu.VMEM((n, piece, 128), BF),
            pltpu.VMEM((n, piece, 128), BF),
            pltpu.VMEM((tokens, features), F32),
            pltpu.VMEM((tokens, 4 * features), F32),
            pltpu.VMEM((tokens, 4 * features), BF),
            pltpu.VMEM((users * HEADS, MAXLEN, MAXLEN), BF),
            pltpu.VMEM((users * HEADS, MAXLEN, MAXLEN), F32),
            pltpu.VMEM((tokens, features), F32),
            pltpu.VMEM((tokens, 4 * features), BF),
            pltpu.VMEM((tokens, features), BF),
            pltpu.VMEM((tokens, features), BF),
            pltpu.SemaphoreType.DMA((8,)),
            pltpu.SemaphoreType.DMA,
            pltpu.SemaphoreType.DMA((4,)),
            pltpu.SemaphoreType.DMA,
            pltpu.SemaphoreType.DMA,
            *ring_scratch(height),
        ],
        compiler_params=pltpu.CompilerParams(
            collective_id=0, has_side_effects=True, vmem_limit_bytes=36 * 2**20
        ),
        name="layer",
    )(
        *(
            pltpu.with_memory_space_constraint(a, pltpu.HBM)
            for a in (ids.reshape(1, tokens), lengths, lines, hot_rows, cold_rows, cot, wu, wo)
        ),
    )


def per_device(item_ids, hot_slot, hot_rows, cold_rows, hist_lengths, out_grad, w_uvqk, w_out):
    grad_scale = 1.0 / math.sqrt(lax.axis_size("bal") * out_grad.shape[0])
    return layer(
        lax.axis_size("table"), grad_scale, item_ids, hot_slot, hot_rows, cold_rows, hist_lengths, out_grad, w_uvqk, w_out
    )


def solution(mesh):
    both = P(("table", "bal"), None)
    return jax.shard_map(
        per_device,
        mesh=mesh,
        in_specs=(P(("table", "bal")), P(), P(), P("table", None), P(), both, P(), P()),
        out_specs=(both, both, both),
        check_vma=False,
    )
```

```python
import functools
import math

import jax
import jax.numpy as jnp
from jax import lax
from jax.experimental import pallas as pl
from jax.experimental.pallas import tpu as pltpu
from jax.sharding import PartitionSpec as P

HEADS = 4
MAXLEN = 128
BF, F32 = jnp.bfloat16, jnp.float32
VMEM = pl.BlockSpec(memory_space=pltpu.VMEM)
HBM = pl.BlockSpec(memory_space=pltpu.HBM)


def dot(a, b, ca=1, cb=0):
    return lax.dot_general(a, b, (((ca,), (cb,)), ((), ())), preferred_element_type=F32)


def iota(shape, dim):
    return lax.broadcasted_iota(jnp.int32, shape, dim)


def one_hot(cond):
    return jnp.where(cond, 1.0, 0.0).astype(BF)


def at_distance(z_count, me, d, do):
    z, core = me // 2, me % 2
    for step, rank, mirrored in ((d, 2 * d - 1, 2 * d), (z_count - d, 2 * d, 2 * d - 1)):
        for c in range(2):
            do(lax.rem(z + step, z_count) * 2 + c, rank * 2 + c, mirrored * 2 + core)


def in_range(z_count, me, low, high, do):
    z, core = me // 2, me % 2
    if high == z_count // 2:
        for c in range(2):
            do(lax.rem(z + high, z_count) * 2 + c, (z_count - 1) * 2 + c, (z_count - 1) * 2 + core)
        high -= 1
    least = max(low, 1)

    def one(i, _):
        at_distance(z_count, me, high - i, do)
        return 0

    lax.fori_loop(0, high - least + 1, one, 0)
    if low == 0:
        do(z * 2 + 1 - core, 1 - core, core)


def ranges(z_count):
    ends = [z_count // 8 - 1, z_count // 4 - 1, 3 * z_count // 8 - 1, z_count // 2]
    low, first, out = 0, 0, []
    for high in ends:
        last = 2 * z_count if high == z_count // 2 else 4 * high + 2
        out.append((low, high, first, last))
        low, first = high + 1, last
    return out


def lookup(
    n, loads, near, meanwhile, ids_ref, slot_ref, hot_ref, cold_ref, ask, asked, wide, found, reply, emb_ref,
    ask_send, ask_recv, reply_send, reply_recv,
):
    z_count = n // 2
    me = lax.axis_index("table")
    z, core = me // 2, me % 2
    batches = ranges(z_count)
    barrier = pltpu.get_barrier_semaphore()

    def greet(peer, mine, theirs):
        pl.semaphore_signal(barrier, inc=1, device_id={"table": peer}, device_id_type=pl.DeviceIdType.MESH)

    in_range(z_count, me, 0, z_count // 2, greet)
    for peer in near:
        pl.semaphore_signal(barrier, inc=1, device_id={"bal": peer}, device_id_type=pl.DeviceIdType.MESH)

    tokens = ids_ref.shape[1]
    per = tokens // n
    shard = cold_ref.shape[0]
    hot_count = hot_ref.shape[0]
    loads[6].wait()
    ids_row = jnp.broadcast_to(ids_ref[...].astype(F32), (tokens, tokens))
    diag = iota((tokens, tokens), 0) == iota((tokens, tokens), 1)
    ids = jnp.sum(jnp.where(diag, ids_row, 0.0), axis=1, keepdims=True).astype(jnp.int32)
    lines = slot_ref.shape[0]
    pick = one_hot(iota((tokens, lines), 1) == ids // 128)
    loads[0].wait()
    slots = slot_ref[...]
    high = dot(pick, (slots // 8).astype(F32).astype(BF))
    low = dot(pick, (slots % 8).astype(F32).astype(BF))
    lane = iota((tokens, 128), 1)
    hot_index = jnp.sum(jnp.where(lane == ids % 128, high * 8.0 + low, 0.0), axis=1, keepdims=True).astype(jnp.int32)
    owner = ids // shard
    row = ids % shard
    away = (owner // 2 - z + z_count) % z_count
    rank = jnp.where(away == 0, 0, jnp.where(away <= z_count // 2, 2 * away - 1, 2 * (z_count - away)))
    owner = rank * 2 + owner % 2
    cold = hot_index >= hot_count
    marks = one_hot((lane == owner) & cold)
    before = dot(one_hot(iota((tokens, tokens), 1) < iota((tokens, tokens), 0)), marks)
    place = jnp.sum(before * marks.astype(F32), axis=1, keepdims=True).astype(jnp.int32)
    digits = jnp.where(
        lane == place, (row // 8).astype(F32), jnp.where(lane == place + per, (row % 8).astype(F32), 0.0)
    ).astype(BF)
    ask[...] = dot(marks, digits, 0, 0)[:n].reshape(n, 1, 128)

    pl.semaphore_wait(barrier, n - 1 + len(near))

    def send(src, dst, low, high, out_sem, in_sem):
        def one(peer, mine, theirs):
            pltpu.make_async_remote_copy(
                src_ref=src.at[mine], dst_ref=dst.at[theirs], send_sem=out_sem, recv_sem=in_sem,
                device_id={"table": peer}, device_id_type=pl.DeviceIdType.MESH,
            ).start()

        in_range(z_count, me, low, high, one)

    def settle(ref, first, last, sem):
        part = ref.at[pl.ds(first, last - first)]
        pltpu.make_async_copy(part, part, sem).wait()

    for k, (low_d, high_d, _, _) in reversed(list(enumerate(batches))):
        send(ask, asked, low_d, high_d, ask_send, ask_recv.at[k])
    asked[core] = ask[core]
    loads[2].wait()
    emb_ref[...] = dot(one_hot(iota((tokens, hot_count), 1) == hot_index), hot_ref[...])
    loads[1].wait()

    pieces = cold_ref.shape[1] // 128
    for k, (low_d, high_d, first, last) in enumerate(batches):
        settle(asked, first + (k == 0), last, ask_recv.at[k])
        count = (last - first) * per
        spread = one_hot(iota((count, last - first), 0) // per == iota((count, last - first), 1))
        got = dot(spread, asked[first:last].reshape(last - first, 128).astype(BF))
        lanes = iota((count, 128), 1)
        turn = iota((count, 128), 0) % per
        want = jnp.sum(
            jnp.where(lanes == turn, got * 8.0, jnp.where(lanes == turn + per, got, 0.0)), axis=1, keepdims=True
        ).astype(jnp.int32)
        rows = dot(one_hot(iota((count, shard), 1) == want), cold_ref[...])
        base = first * per * pieces
        for j in range(pieces):
            wide[pl.ds(base + j, count, stride=pieces), :] = rows[:, j * 128 : (j + 1) * 128]
        found[first:last] = (
            wide[base : base + count * pieces].astype(BF).reshape(last - first, per * pieces, 128)
        )
        send(found, reply, low_d, high_d, reply_send, reply_recv)
        if k == 0:
            reply[core] = found[core]
    take = one_hot(iota((tokens, tokens), 1) == jnp.where(cold, owner * per + place, -1))
    meanwhile()
    settle(reply, 1, n, reply_recv)

    wide[...] = reply[...].reshape(wide.shape).astype(F32)
    for j in range(pieces):
        cut = slice(j * 128, (j + 1) * 128)
        piece = wide[pl.ds(j, tokens, stride=pieces), :].astype(BF)
        emb_ref[:, cut] += dot(take, piece)

    def end():
        settle(ask, 1, n, ask_send)
        settle(found, 1, n, reply_send)

    return end


def normalised(values):
    mean = jnp.mean(values, axis=-1, keepdims=True)
    centred = values - mean
    scale = lax.rsqrt(jnp.mean(centred * centred, axis=-1, keepdims=True) + 1e-05)
    return centred * scale, scale


def silu_both(v):
    sig = 0.5 * jnp.tanh(0.5 * v) + 0.5
    act = v * sig
    return act, sig + act * (1.0 - sig)


WIDE = 256
GROUPS = ((4, 0), (1, 2, 3))


class Ring:
    def __init__(self, send1, recv1, send2, recv2, *refs):
        count = len(GROUPS)
        self.g, self.in1, self.out1, self.total, self.tot_bf, self.in2, self.out2 = (
            refs[k * count : (k + 1) * count] for k in range(7)
        )
        self.sems = ((send1, recv1), (send2, recv2))
        me = lax.axis_index("bal")
        x, y = me // 4, me % 4
        self.places = ((x, y), (y, x))
        along_x = tuple((x + step) % 4 * 4 + y for step in (1, 3))
        along_y = tuple(x * 4 + (y + step) % 4 for step in (1, 3))
        self.peers = ((along_x, along_y), (along_y, along_x))
        self.near = (*along_x, *along_y)
        self.sent = {}

    def post(self, stage, c, half, way, msg):
        at = self.places[half][stage]
        step = (1, 3)[way]
        if stage == 0:
            mine, other = pl.ds(2 * way, 2), pl.ds(2 - 2 * way, 2)
            src, land, out = self.g, self.in1, self.out1
        else:
            mid = self.tot_bf[c].shape[2] // 2
            mine, other = pl.ds(mid * way, mid), pl.ds(mid - mid * way, mid)
            src, land, out = self.tot_bf, self.in2, self.out2
        ref = (
            src[c].at[half, (at + 2) % 4, mine],
            src[c].at[half, (at + step) % 4, other],
            out[c].at[half, way],
        )[msg]
        send, recv = self.sems[stage]
        copy = pltpu.make_async_remote_copy(
            src_ref=ref, dst_ref=land[c].at[half, way, msg],
            send_sem=send.at[c, half, way, msg], recv_sem=recv.at[c, half, way, msg],
            device_id={"bal": self.peers[half][stage][way]}, device_id_type=pl.DeviceIdType.MESH,
        )
        copy.start()
        self.sent[stage, c, half, way, msg] = copy

    def arrive(self, stage, c, half, way, msg):
        self.sent[stage, c, half, way, msg].wait_recv()

    def start(self, stage, c):
        for msg in (0, 1):
            for half in range(2):
                for way in range(2):
                    self.post(stage, c, half, way, msg)

    def relay(self, stage, c):
        for half in range(2):
            at = self.places[half][stage]
            for way in range(2):
                self.arrive(stage, c, half, way, 0)
                to = (at + (1, 3)[way]) % 4
                if stage == 0:
                    own = self.g[c][half, to, pl.ds(2 * way, 2)].astype(F32)
                    self.out1[c][half, way] = (own + self.in1[c][half, way, 0].astype(F32)).astype(BF)
                else:
                    mid = self.tot_bf[c].shape[2] // 2
                    own = self.total[c][half, to, pl.ds(mid * way, mid)]
                    self.out2[c][half, way] = (own + self.in2[c][half, way, 0].astype(F32)).astype(BF)
                self.post(stage, c, half, way, 2)

    def turn(self, c):
        for half in range(2):
            a = self.places[half][0]
            for way in range(2):
                self.arrive(0, c, half, way, 1)
                self.arrive(0, c, half, way, 2)
            for part in range(2):
                here = pl.ds(2 * part, 2)
                t = (
                    self.g[c][half, a, here].astype(F32)
                    + self.in1[c][half, part, 2].astype(F32)
                    + self.in1[c][half, 1 - part, 1].astype(F32)
                )
                self.total[c][half, here] = t
                self.tot_bf[c][half, here] = t.astype(BF)
        self.start(1, c)

    def finish(self, c, store):
        mid = self.tot_bf[c].shape[2] // 2
        for half in range(2):
            b = self.places[half][1]
            for way in range(2):
                self.arrive(1, c, half, way, 1)
                self.arrive(1, c, half, way, 2)
            for part in range(2):
                rows = pl.ds(mid * part, mid)
                store(
                    c, half, rows,
                    self.total[c][half, b, rows]
                    + self.in2[c][half, part, 2].astype(F32)
                    + self.in2[c][half, 1 - part, 1].astype(F32),
                )

    def drain(self):
        for copy in self.sent.values():
            copy.wait_send()


def layer_kernel(
    n_table, grad_scale, ids_hbm, len_hbm, slot_hbm, hot_hbm, cold_hbm, cot_hbm, wu_hbm, wo_hbm,
    out_ref, first_ref, second_ref,
    ids_ref, len_ref, slot_ref, hot_ref, cold_ref, cot_ref, wu_ref, wo_ref, ask, asked, wide, found, reply, emb_ref,
    slope, acts, attn, attn_slope, mixed, grads, signal_ref, back_ref,
    load_sem, ask_send, ask_recv, reply_send, reply_recv, *ring_refs,
):
    tokens, features = emb_ref.shape
    loads = [
        pltpu.make_async_copy(src, dst, load_sem.at[k])
        for k, (src, dst) in enumerate((
            (slot_hbm, slot_ref), (cold_hbm, cold_ref), (hot_hbm, hot_ref),
            (cot_hbm, cot_ref), (wo_hbm, wo_ref), (wu_hbm, wu_ref), (ids_hbm, ids_ref), (len_hbm, len_ref),
        ))
    ]
    for k in (6, 7, 0, 1, 2, 3, 4, 5):
        loads[k].start()
    ring = Ring(*ring_refs)
    users = tokens // MAXLEN
    head = features // HEADS
    first = (lax.axis_index("table") * lax.axis_size("bal") + lax.axis_index("bal")) * users

    def valid_below():
        return [len_ref[first + u] for u in range(users)]

    def cotangent():
        for load in loads[3:6] + loads[7:]:
            load.wait()
        lengths = valid_below()
        at = iota((tokens, 1), 0)
        ends = jnp.full((tokens, 1), lengths[0], jnp.int32)
        for u in range(1, users):
            ends = jnp.where(at >= u * MAXLEN, u * MAXLEN + lengths[u], ends)
        signal = (jnp.where(at < ends, cot_ref[...].astype(F32), 0.0) * grad_scale).astype(BF)
        signal_ref[...] = signal
        back_ref[...] = dot(signal, wo_ref[...], 1, 1).astype(BF)

    end = lookup(
        n_table, loads, ring.near, cotangent, ids_ref, slot_ref, hot_ref, cold_ref, ask, asked, wide, found, reply,
        emb_ref, ask_send, ask_recv, reply_send, reply_recv,
    )
    emb = emb_ref[...]
    normed = normalised(emb)[0].astype(BF)
    for b in (2, 3, 1, 0):
        cut = slice(b * features, (b + 1) * features)
        act, dact = silu_both(dot(normed, wu_ref[:, cut]))
        acts[:, cut] = act.astype(BF)
        slope[:, cut] = dact
    lengths = valid_below()
    i, j = iota((MAXLEN, MAXLEN), 0), iota((MAXLEN, MAXLEN), 1)
    scale = 1.0 / math.sqrt(head)

    def part(b, u, h):
        at = b * features + h * head
        return acts[u * MAXLEN : (u + 1) * MAXLEN, at : at + head]

    for u in range(users):
        allowed = (j <= i) & (i < lengths[u])
        for h in range(HEADS):
            s = dot(part(2, u, h), part(3, u, h), 1, 1) * scale
            act, dact = silu_both(s)
            w = jnp.where(allowed, act, 0.0).astype(BF)
            attn[u * HEADS + h] = w
            attn_slope[u * HEADS + h] = jnp.where(allowed, dact * scale, 0.0)
            mixed[u * MAXLEN : (u + 1) * MAXLEN, h * head : (h + 1) * head] = dot(w, part(1, u, h))

    n, rstd = normalised(mixed[...])
    gate = acts[:, :features].astype(F32)
    gated = (n * gate).astype(BF)
    signal = signal_ref[...]

    def spread(block, left, right):
        [c] = [c for c, group in enumerate(GROUPS) if block in group]
        at = GROUPS[c].index(block) * WIDE
        height = features // 16
        for half in range(2):
            value = dot(left, right[:, half * WIDE : (half + 1) * WIDE], 0, 0).astype(BF)
            for b in range(16):
                x, y = divmod(b, 4)
                f, s = (x, y) if half == 0 else (y, x)
                ring.g[c][half, f, s, :, at : at + WIDE] = value[b * height : (b + 1) * height]
        if block == GROUPS[c][-1]:
            ring.start(0, c)

    spread(4, gated, signal)
    back = back_ref[...].astype(F32)
    grads[:, :features] = ((back * n).astype(BF).astype(F32) * slope[:, :features]).astype(BF)
    spread(0, normed, grads[:, :features])
    dn = back * gate
    mixed[...] = rstd * (
        dn - jnp.mean(dn, axis=-1, keepdims=True) - n * jnp.mean(dn * n, axis=-1, keepdims=True)
    )
    for u in range(users):
        rows = slice(u * MAXLEN, (u + 1) * MAXLEN)
        for h in range(HEADS):
            dm = mixed[rows, h * head : (h + 1) * head].astype(BF)
            w = attn[u * HEADS + h]
            dw = dot(dm, part(1, u, h), 1, 1).astype(BF).astype(F32)
            ds = (dw * attn_slope[u * HEADS + h]).astype(BF)
            for b, d in (
                (1, dot(w, dm, 0, 0)),
                (2, dot(ds, part(3, u, h))),
                (3, dot(ds, part(2, u, h), 0, 0)),
            ):
                cols = slice(b * features + h * head, b * features + (h + 1) * head)
                grads[rows, cols] = (d.astype(BF).astype(F32) * slope[rows, cols]).astype(BF)
    for b in range(1, 4):
        spread(b, normed, grads[:, b * features : (b + 1) * features])

    def store(c, half, rows, value):
        for k, block in enumerate(GROUPS[c]):
            piece = value[:, k * WIDE : (k + 1) * WIDE]
            low = half * WIDE
            if block == 4:
                second_ref[rows, low : low + WIDE] = piece
            else:
                first_ref[rows, block * features + low : block * features + low + WIDE] = piece

    chunks = range(len(GROUPS))
    for c in chunks:
        ring.relay(0, c)
    out_ref[...] = (emb + dot(gated, wo_ref[...])).astype(BF)
    for c in chunks:
        ring.turn(c)
    for c in chunks:
        ring.relay(1, c)
    for c in chunks:
        ring.finish(c, store)
    ring.drain()
    end()


def ring_scratch(height):
    dma = pltpu.SemaphoreType.DMA((len(GROUPS), 2, 2, 3))
    shapes = (
        ((2, 4, 4, height), BF),
        ((2, 2, 3, 2, height), BF),
        ((2, 2, 2, height), BF),
        ((2, 4, height), F32),
        ((2, 4, height), BF),
        ((2, 2, 3, height // 2), BF),
        ((2, 2, height // 2), BF),
    )
    return [dma] * 4 + [
        pltpu.VMEM((*shape, WIDE * len(group)), kind) for shape, kind in shapes for group in GROUPS
    ]


def layer(n, grad_scale, ids, hot_slot, hot_rows, cold_rows, lengths, cot, wu, wo):
    tokens, features = cot.shape
    users = tokens // MAXLEN
    height = features // 16
    piece = features // 128 * (tokens // n)
    lines = hot_slot.reshape(-1, 128)
    return pl.pallas_call(
        functools.partial(layer_kernel, n, grad_scale),
        out_shape=(
            jax.ShapeDtypeStruct((tokens, features), BF),
            jax.ShapeDtypeStruct((height, 4 * features), F32),
            jax.ShapeDtypeStruct((height, features), F32),
        ),
        in_specs=[HBM] * 8,
        out_specs=(VMEM, VMEM, VMEM),
        scratch_shapes=[
            pltpu.VMEM((1, tokens), jnp.int32),
            pltpu.SMEM(lengths.shape, jnp.int32),
            pltpu.VMEM(lines.shape, jnp.int32),
            pltpu.VMEM(hot_rows.shape, BF),
            pltpu.VMEM(cold_rows.shape, BF),
            pltpu.VMEM(cot.shape, BF),
            pltpu.VMEM(wu.shape, BF),
            pltpu.VMEM(wo.shape, BF),
            pltpu.VMEM((n, 1, 128), F32),
            pltpu.VMEM((n, 1, 128), F32),
            pltpu.VMEM((n * piece, 128), F32),
            pltpu.VMEM((n, piece, 128), BF),
            pltpu.VMEM((n, piece, 128), BF),
            pltpu.VMEM((tokens, features), F32),
            pltpu.VMEM((tokens, 4 * features), F32),
            pltpu.VMEM((tokens, 4 * features), BF),
            pltpu.VMEM((users * HEADS, MAXLEN, MAXLEN), BF),
            pltpu.VMEM((users * HEADS, MAXLEN, MAXLEN), F32),
            pltpu.VMEM((tokens, features), F32),
            pltpu.VMEM((tokens, 4 * features), BF),
            pltpu.VMEM((tokens, features), BF),
            pltpu.VMEM((tokens, features), BF),
            pltpu.SemaphoreType.DMA((8,)),
            pltpu.SemaphoreType.DMA,
            pltpu.SemaphoreType.DMA((4,)),
            pltpu.SemaphoreType.DMA,
            pltpu.SemaphoreType.DMA,
            *ring_scratch(height),
        ],
        compiler_params=pltpu.CompilerParams(
            collective_id=0, has_side_effects=True, vmem_limit_bytes=36 * 2**20
        ),
        name="layer",
    )(
        *(
            pltpu.with_memory_space_constraint(a, pltpu.HBM)
            for a in (ids.reshape(1, tokens), lengths, lines, hot_rows, cold_rows, cot, wu, wo)
        ),
    )


def put_kernel(*refs):
    count = len(refs) // 2
    copies = [pltpu.make_async_copy(refs[k], refs[count + k], refs[-1].at[k]) for k in range(count)]
    for copy in copies:
        copy.start()
    for copy in copies:
        copy.wait()


def put(*arrays):
    return pl.pallas_call(
        put_kernel,
        out_shape=tuple(jax.ShapeDtypeStruct(a.shape, a.dtype) for a in arrays),
        in_specs=[VMEM] * len(arrays),
        out_specs=(HBM,) * len(arrays),
        scratch_shapes=[pltpu.SemaphoreType.DMA((len(arrays),))],
        name="put",
    )(*(pltpu.with_memory_space_constraint(a, pltpu.VMEM) for a in arrays))


def per_device(item_ids, hot_slot, hot_rows, cold_rows, hist_lengths, out_grad, w_uvqk, w_out):
    grad_scale = 1.0 / math.sqrt(lax.axis_size("bal") * out_grad.shape[0])
    return put(*layer(
        lax.axis_size("table"), grad_scale, item_ids, hot_slot, hot_rows, cold_rows, hist_lengths, out_grad, w_uvqk, w_out
    ))


def solution(mesh):
    both = P(("table", "bal"), None)
    return jax.shard_map(
        per_device,
        mesh=mesh,
        in_specs=(P(("table", "bal")), P(), P(), P("table", None), P(), both, P(), P()),
        out_specs=(both, both, both),
        check_vma=False,
    )
```

```python
import functools
import math

import jax
import jax.numpy as jnp
from jax import lax
from jax.experimental import pallas as pl
from jax.experimental.pallas import tpu as pltpu
from jax.sharding import PartitionSpec as P

HEADS = 4
MAXLEN = 128
BF, F32 = jnp.bfloat16, jnp.float32
VMEM = pl.BlockSpec(memory_space=pltpu.VMEM)
HBM = pl.BlockSpec(memory_space=pltpu.HBM)


def dot(a, b, ca=1, cb=0):
    return lax.dot_general(a, b, (((ca,), (cb,)), ((), ())), preferred_element_type=F32)


def iota(shape, dim):
    return lax.broadcasted_iota(jnp.int32, shape, dim)


def one_hot(cond):
    return jnp.where(cond, 1.0, 0.0).astype(BF)


def at_distance(z_count, me, d, do):
    z, core = me // 2, me % 2
    for step, rank, mirrored in ((d, 2 * d - 1, 2 * d), (z_count - d, 2 * d, 2 * d - 1)):
        for c in range(2):
            do(lax.rem(z + step, z_count) * 2 + c, rank * 2 + c, mirrored * 2 + core)


def in_range(z_count, me, low, high, do):
    z, core = me // 2, me % 2
    if high == z_count // 2:
        for c in range(2):
            do(lax.rem(z + high, z_count) * 2 + c, (z_count - 1) * 2 + c, (z_count - 1) * 2 + core)
        high -= 1
    least = max(low, 1)

    def one(i, _):
        at_distance(z_count, me, high - i, do)
        return 0

    lax.fori_loop(0, high - least + 1, one, 0)
    if low == 0:
        do(z * 2 + 1 - core, 1 - core, core)


def ranges(z_count):
    ends = [z_count // 8 - 1, z_count // 4 - 1, 3 * z_count // 8 - 1, z_count // 2]
    low, first, out = 0, 0, []
    for high in ends:
        last = 2 * z_count if high == z_count // 2 else 4 * high + 2
        out.append((low, high, first, last))
        low, first = high + 1, last
    return out


def lookup(
    n, loads, near, meanwhile, ids_ref, slot_ref, hot_ref, cold_ref, ask, asked, wide, found, reply, emb_ref,
    ask_send, ask_recv, reply_send, reply_recv,
):
    z_count = n // 2
    me = lax.axis_index("table")
    z, core = me // 2, me % 2
    batches = ranges(z_count)
    barrier = pltpu.get_barrier_semaphore()

    def greet(peer, mine, theirs):
        pl.semaphore_signal(barrier, inc=1, device_id={"table": peer}, device_id_type=pl.DeviceIdType.MESH)

    in_range(z_count, me, 0, z_count // 2, greet)
    for peer in near:
        pl.semaphore_signal(barrier, inc=1, device_id={"bal": peer}, device_id_type=pl.DeviceIdType.MESH)

    tokens = ids_ref.shape[1]
    per = tokens // n
    shard = cold_ref.shape[0]
    hot_count = hot_ref.shape[0]
    loads[6].wait()
    ids_row = jnp.broadcast_to(ids_ref[...].astype(F32), (tokens, tokens))
    diag = iota((tokens, tokens), 0) == iota((tokens, tokens), 1)
    ids = jnp.sum(jnp.where(diag, ids_row, 0.0), axis=1, keepdims=True).astype(jnp.int32)
    lines = slot_ref.shape[0]
    pick = one_hot(iota((tokens, lines), 1) == ids // 128)
    loads[0].wait()
    slots = slot_ref[...]
    high = dot(pick, (slots // 8).astype(F32).astype(BF))
    low = dot(pick, (slots % 8).astype(F32).astype(BF))
    lane = iota((tokens, 128), 1)
    hot_index = jnp.sum(jnp.where(lane == ids % 128, high * 8.0 + low, 0.0), axis=1, keepdims=True).astype(jnp.int32)
    owner = ids // shard
    row = ids % shard
    away = (owner // 2 - z + z_count) % z_count
    rank = jnp.where(away == 0, 0, jnp.where(away <= z_count // 2, 2 * away - 1, 2 * (z_count - away)))
    owner = rank * 2 + owner % 2
    cold = hot_index >= hot_count
    marks = one_hot((lane == owner) & cold)
    before = dot(one_hot(iota((tokens, tokens), 1) < iota((tokens, tokens), 0)), marks)
    place = jnp.sum(before * marks.astype(F32), axis=1, keepdims=True).astype(jnp.int32)
    digits = jnp.where(
        lane == place, (row // 8).astype(F32), jnp.where(lane == place + per, (row % 8).astype(F32), 0.0)
    ).astype(BF)
    ask[...] = dot(marks, digits, 0, 0)[:n].reshape(n, 1, 128)

    pl.semaphore_wait(barrier, n - 1 + len(near))

    def send(src, dst, low, high, out_sem, in_sem):
        def one(peer, mine, theirs):
            pltpu.make_async_remote_copy(
                src_ref=src.at[mine], dst_ref=dst.at[theirs], send_sem=out_sem, recv_sem=in_sem,
                device_id={"table": peer}, device_id_type=pl.DeviceIdType.MESH,
            ).start()

        in_range(z_count, me, low, high, one)

    def settle(ref, first, last, sem):
        part = ref.at[pl.ds(first, last - first)]
        pltpu.make_async_copy(part, part, sem).wait()

    for k, (low_d, high_d, _, _) in reversed(list(enumerate(batches))):
        send(ask, asked, low_d, high_d, ask_send, ask_recv.at[k])
    asked[core] = ask[core]
    loads[2].wait()
    emb_ref[...] = dot(one_hot(iota((tokens, hot_count), 1) == hot_index), hot_ref[...])
    loads[1].wait()

    pieces = cold_ref.shape[1] // 128
    for k, (low_d, high_d, first, last) in enumerate(batches):
        settle(asked, first + (k == 0), last, ask_recv.at[k])
        count = (last - first) * per
        spread = one_hot(iota((count, last - first), 0) // per == iota((count, last - first), 1))
        got = dot(spread, asked[first:last].reshape(last - first, 128).astype(BF))
        lanes = iota((count, 128), 1)
        turn = iota((count, 128), 0) % per
        want = jnp.sum(
            jnp.where(lanes == turn, got * 8.0, jnp.where(lanes == turn + per, got, 0.0)), axis=1, keepdims=True
        ).astype(jnp.int32)
        rows = dot(one_hot(iota((count, shard), 1) == want), cold_ref[...])
        base = first * per * pieces
        for j in range(pieces):
            wide[pl.ds(base + j, count, stride=pieces), :] = rows[:, j * 128 : (j + 1) * 128]
        found[first:last] = (
            wide[base : base + count * pieces].astype(BF).reshape(last - first, per * pieces, 128)
        )
        send(found, reply, low_d, high_d, reply_send, reply_recv)
        if k == 0:
            reply[core] = found[core]
    take = one_hot(iota((tokens, tokens), 1) == jnp.where(cold, owner * per + place, -1))
    meanwhile()
    settle(reply, 1, n, reply_recv)

    wide[...] = reply[...].reshape(wide.shape).astype(F32)
    for j in range(pieces):
        cut = slice(j * 128, (j + 1) * 128)
        piece = wide[pl.ds(j, tokens, stride=pieces), :].astype(BF)
        emb_ref[:, cut] += dot(take, piece)

    def end():
        settle(ask, 1, n, ask_send)
        settle(found, 1, n, reply_send)

    return end


def normalised(values):
    mean = jnp.mean(values, axis=-1, keepdims=True)
    centred = values - mean
    scale = lax.rsqrt(jnp.mean(centred * centred, axis=-1, keepdims=True) + 1e-05)
    return centred * scale, scale


def silu_both(v):
    sig = 0.5 * jnp.tanh(0.5 * v) + 0.5
    act = v * sig
    return act, sig + act * (1.0 - sig)


WIDE = 256
GROUPS = ((4, 0), (1, 2, 3))


class Ring:
    def __init__(self, send1, recv1, send2, recv2, *refs):
        count = len(GROUPS)
        self.g, self.in1, self.out1, self.total, self.tot_bf, self.in2, self.out2 = (
            refs[k * count : (k + 1) * count] for k in range(7)
        )
        self.sems = ((send1, recv1), (send2, recv2))
        me = lax.axis_index("bal")
        x, y = me // 4, me % 4
        self.places = ((x, y), (y, x))
        along_x = tuple((x + step) % 4 * 4 + y for step in (1, 3))
        along_y = tuple(x * 4 + (y + step) % 4 for step in (1, 3))
        self.peers = ((along_x, along_y), (along_y, along_x))
        self.near = (*along_x, *along_y)
        self.sent = {}

    def post(self, stage, c, half, way, msg):
        at = self.places[half][stage]
        step = (1, 3)[way]
        if stage == 0:
            mine, other = pl.ds(2 * way, 2), pl.ds(2 - 2 * way, 2)
            src, land, out = self.g, self.in1, self.out1
        else:
            mid = self.tot_bf[c].shape[2] // 2
            mine, other = pl.ds(mid * way, mid), pl.ds(mid - mid * way, mid)
            src, land, out = self.tot_bf, self.in2, self.out2
        ref = (
            src[c].at[half, (at + 2) % 4, mine],
            src[c].at[half, (at + step) % 4, other],
            out[c].at[half, way],
        )[msg]
        send, recv = self.sems[stage]
        copy = pltpu.make_async_remote_copy(
            src_ref=ref, dst_ref=land[c].at[half, way, msg],
            send_sem=send.at[c, half, way, msg], recv_sem=recv.at[c, half, way, msg],
            device_id={"bal": self.peers[half][stage][way]}, device_id_type=pl.DeviceIdType.MESH,
        )
        copy.start()
        self.sent[stage, c, half, way, msg] = copy

    def arrive(self, stage, c, half, way, msg):
        self.sent[stage, c, half, way, msg].wait_recv()

    def start(self, stage, c):
        for msg in (0, 1):
            for half in range(2):
                for way in range(2):
                    self.post(stage, c, half, way, msg)

    def relay(self, stage, c):
        for half in range(2):
            at = self.places[half][stage]
            for way in range(2):
                self.arrive(stage, c, half, way, 0)
                to = (at + (1, 3)[way]) % 4
                if stage == 0:
                    own = self.g[c][half, to, pl.ds(2 * way, 2)].astype(F32)
                    self.out1[c][half, way] = (own + self.in1[c][half, way, 0].astype(F32)).astype(BF)
                else:
                    mid = self.tot_bf[c].shape[2] // 2
                    own = self.total[c][half, to, pl.ds(mid * way, mid)]
                    self.out2[c][half, way] = (own + self.in2[c][half, way, 0].astype(F32)).astype(BF)
                self.post(stage, c, half, way, 2)

    def turn(self, c):
        for half in range(2):
            a = self.places[half][0]
            for way in range(2):
                self.arrive(0, c, half, way, 1)
                self.arrive(0, c, half, way, 2)
            for part in range(2):
                here = pl.ds(2 * part, 2)
                t = (
                    self.g[c][half, a, here].astype(F32)
                    + self.in1[c][half, part, 2].astype(F32)
                    + self.in1[c][half, 1 - part, 1].astype(F32)
                )
                self.total[c][half, here] = t
                self.tot_bf[c][half, here] = t.astype(BF)
        self.start(1, c)

    def finish(self, c, store):
        mid = self.tot_bf[c].shape[2] // 2
        for half in range(2):
            b = self.places[half][1]
            for way in range(2):
                self.arrive(1, c, half, way, 1)
                self.arrive(1, c, half, way, 2)
            for part in range(2):
                rows = pl.ds(mid * part, mid)
                store(
                    c, half, rows,
                    self.total[c][half, b, rows]
                    + self.in2[c][half, part, 2].astype(F32)
                    + self.in2[c][half, 1 - part, 1].astype(F32),
                )

    def drain(self, stage):
        for key, copy in self.sent.items():
            if key[0] == stage:
                copy.wait_send()


def layer_kernel(
    n_table, grad_scale, ids_hbm, len_hbm, slot_hbm, hot_hbm, cold_hbm, cot_hbm, wu_hbm, wo_hbm,
    out_ref, first_ref, second_ref,
    ids_ref, len_ref, slot_ref, hot_ref, cold_ref, cot_ref, wu_ref, wo_ref, ask, asked, wide, found, reply, emb_ref,
    slope, acts, attn, attn_slope, mixed, grads, signal_ref, back_ref,
    load_sem, ask_send, ask_recv, reply_send, reply_recv, *ring_refs,
):
    tokens, features = emb_ref.shape
    loads = [
        pltpu.make_async_copy(src, dst, load_sem.at[k])
        for k, (src, dst) in enumerate((
            (slot_hbm, slot_ref), (cold_hbm, cold_ref), (hot_hbm, hot_ref),
            (cot_hbm, cot_ref), (wo_hbm, wo_ref), (wu_hbm, wu_ref), (ids_hbm, ids_ref), (len_hbm, len_ref),
        ))
    ]
    for k in (6, 7, 0, 1, 2, 3, 4, 5):
        loads[k].start()
    ring = Ring(*ring_refs)
    users = tokens // MAXLEN
    head = features // HEADS
    first = (lax.axis_index("table") * lax.axis_size("bal") + lax.axis_index("bal")) * users

    def valid_below():
        return [len_ref[first + u] for u in range(users)]

    def cotangent():
        for load in loads[3:6] + loads[7:]:
            load.wait()
        lengths = valid_below()
        at = iota((tokens, 1), 0)
        ends = jnp.full((tokens, 1), lengths[0], jnp.int32)
        for u in range(1, users):
            ends = jnp.where(at >= u * MAXLEN, u * MAXLEN + lengths[u], ends)
        signal = (jnp.where(at < ends, cot_ref[...].astype(F32), 0.0) * grad_scale).astype(BF)
        signal_ref[...] = signal
        back_ref[...] = dot(signal, wo_ref[...], 1, 1).astype(BF)

    end = lookup(
        n_table, loads, ring.near, cotangent, ids_ref, slot_ref, hot_ref, cold_ref, ask, asked, wide, found, reply,
        emb_ref, ask_send, ask_recv, reply_send, reply_recv,
    )
    emb = emb_ref[...]
    normed = normalised(emb)[0].astype(BF)
    for b in (2, 3, 1, 0):
        cut = slice(b * features, (b + 1) * features)
        act, dact = silu_both(dot(normed, wu_ref[:, cut]))
        acts[:, cut] = act.astype(BF)
        slope[:, cut] = dact
    lengths = valid_below()
    i, j = iota((MAXLEN, MAXLEN), 0), iota((MAXLEN, MAXLEN), 1)
    scale = 1.0 / math.sqrt(head)

    def part(b, u, h):
        at = b * features + h * head
        return acts[u * MAXLEN : (u + 1) * MAXLEN, at : at + head]

    for u in range(users):
        allowed = (j <= i) & (i < lengths[u])
        for h in range(HEADS):
            s = dot(part(2, u, h), part(3, u, h), 1, 1) * scale
            act, dact = silu_both(s)
            w = jnp.where(allowed, act, 0.0).astype(BF)
            attn[u * HEADS + h] = w
            attn_slope[u * HEADS + h] = jnp.where(allowed, dact * scale, 0.0)
            mixed[u * MAXLEN : (u + 1) * MAXLEN, h * head : (h + 1) * head] = dot(w, part(1, u, h))

    n, rstd = normalised(mixed[...])
    gate = acts[:, :features].astype(F32)
    gated = (n * gate).astype(BF)
    signal = signal_ref[...]

    def spread(block, left, right):
        [c] = [c for c, group in enumerate(GROUPS) if block in group]
        at = GROUPS[c].index(block) * WIDE
        height = features // 16
        for half in range(2):
            value = dot(left, right[:, half * WIDE : (half + 1) * WIDE], 0, 0).astype(BF)
            for b in range(16):
                x, y = divmod(b, 4)
                f, s = (x, y) if half == 0 else (y, x)
                ring.g[c][half, f, s, :, at : at + WIDE] = value[b * height : (b + 1) * height]
        if block == GROUPS[c][-1]:
            ring.start(0, c)

    spread(4, gated, signal)
    back = back_ref[...].astype(F32)
    grads[:, :features] = ((back * n).astype(BF).astype(F32) * slope[:, :features]).astype(BF)
    spread(0, normed, grads[:, :features])
    dn = back * gate
    mixed[...] = rstd * (
        dn - jnp.mean(dn, axis=-1, keepdims=True) - n * jnp.mean(dn * n, axis=-1, keepdims=True)
    )
    for u in range(users):
        rows = slice(u * MAXLEN, (u + 1) * MAXLEN)
        for h in range(HEADS):
            dm = mixed[rows, h * head : (h + 1) * head].astype(BF)
            w = attn[u * HEADS + h]
            dw = dot(dm, part(1, u, h), 1, 1).astype(BF).astype(F32)
            ds = (dw * attn_slope[u * HEADS + h]).astype(BF)
            for b, d in (
                (1, dot(w, dm, 0, 0)),
                (2, dot(ds, part(3, u, h))),
                (3, dot(ds, part(2, u, h), 0, 0)),
            ):
                cols = slice(b * features + h * head, b * features + (h + 1) * head)
                grads[rows, cols] = (d.astype(BF).astype(F32) * slope[rows, cols]).astype(BF)
    for b in range(1, 4):
        spread(b, normed, grads[:, b * features : (b + 1) * features])

    def store(c, half, rows, value):
        for k, block in enumerate(GROUPS[c]):
            piece = value[:, k * WIDE : (k + 1) * WIDE]
            low = half * WIDE
            if block == 4:
                second_ref[rows, low : low + WIDE] = piece
            else:
                first_ref[rows, block * features + low : block * features + low + WIDE] = piece

    chunks = range(len(GROUPS))
    for c in chunks:
        ring.relay(0, c)
    out_ref[...] = (emb + dot(gated, wo_ref[...])).astype(BF)
    for c in chunks:
        ring.turn(c)
    ring.drain(0)
    end()
    for c in chunks:
        ring.relay(1, c)
    for c in chunks:
        ring.finish(c, store)
    ring.drain(1)


def ring_scratch(height):
    dma = pltpu.SemaphoreType.DMA((len(GROUPS), 2, 2, 3))
    shapes = (
        ((2, 4, 4, height), BF),
        ((2, 2, 3, 2, height), BF),
        ((2, 2, 2, height), BF),
        ((2, 4, height), F32),
        ((2, 4, height), BF),
        ((2, 2, 3, height // 2), BF),
        ((2, 2, height // 2), BF),
    )
    return [dma] * 4 + [
        pltpu.VMEM((*shape, WIDE * len(group)), kind) for shape, kind in shapes for group in GROUPS
    ]


def layer(n, grad_scale, ids, hot_slot, hot_rows, cold_rows, lengths, cot, wu, wo):
    tokens, features = cot.shape
    users = tokens // MAXLEN
    height = features // 16
    piece = features // 128 * (tokens // n)
    lines = hot_slot.reshape(-1, 128)
    return pl.pallas_call(
        functools.partial(layer_kernel, n, grad_scale),
        out_shape=(
            jax.ShapeDtypeStruct((tokens, features), BF),
            jax.ShapeDtypeStruct((height, 4 * features), F32),
            jax.ShapeDtypeStruct((height, features), F32),
        ),
        in_specs=[HBM] * 8,
        out_specs=(VMEM, VMEM, VMEM),
        scratch_shapes=[
            pltpu.VMEM((1, tokens), jnp.int32),
            pltpu.SMEM(lengths.shape, jnp.int32),
            pltpu.VMEM(lines.shape, jnp.int32),
            pltpu.VMEM(hot_rows.shape, BF),
            pltpu.VMEM(cold_rows.shape, BF),
            pltpu.VMEM(cot.shape, BF),
            pltpu.VMEM(wu.shape, BF),
            pltpu.VMEM(wo.shape, BF),
            pltpu.VMEM((n, 1, 128), F32),
            pltpu.VMEM((n, 1, 128), F32),
            pltpu.VMEM((n * piece, 128), F32),
            pltpu.VMEM((n, piece, 128), BF),
            pltpu.VMEM((n, piece, 128), BF),
            pltpu.VMEM((tokens, features), F32),
            pltpu.VMEM((tokens, 4 * features), F32),
            pltpu.VMEM((tokens, 4 * features), BF),
            pltpu.VMEM((users * HEADS, MAXLEN, MAXLEN), BF),
            pltpu.VMEM((users * HEADS, MAXLEN, MAXLEN), F32),
            pltpu.VMEM((tokens, features), F32),
            pltpu.VMEM((tokens, 4 * features), BF),
            pltpu.VMEM((tokens, features), BF),
            pltpu.VMEM((tokens, features), BF),
            pltpu.SemaphoreType.DMA((8,)),
            pltpu.SemaphoreType.DMA,
            pltpu.SemaphoreType.DMA((4,)),
            pltpu.SemaphoreType.DMA,
            pltpu.SemaphoreType.DMA,
            *ring_scratch(height),
        ],
        compiler_params=pltpu.CompilerParams(
            collective_id=0, has_side_effects=True, vmem_limit_bytes=36 * 2**20
        ),
        name="layer",
    )(
        *(
            pltpu.with_memory_space_constraint(a, pltpu.HBM)
            for a in (ids.reshape(1, tokens), lengths, lines, hot_rows, cold_rows, cot, wu, wo)
        ),
    )


def put_kernel(*refs):
    count = len(refs) // 2
    copies = [pltpu.make_async_copy(refs[k], refs[count + k], refs[-1].at[k]) for k in range(count)]
    for copy in copies:
        copy.start()
    for copy in copies:
        copy.wait()


def put(*arrays):
    return pl.pallas_call(
        put_kernel,
        out_shape=tuple(jax.ShapeDtypeStruct(a.shape, a.dtype) for a in arrays),
        in_specs=[VMEM] * len(arrays),
        out_specs=(HBM,) * len(arrays),
        scratch_shapes=[pltpu.SemaphoreType.DMA((len(arrays),))],
        name="put",
    )(*(pltpu.with_memory_space_constraint(a, pltpu.VMEM) for a in arrays))


def per_device(item_ids, hot_slot, hot_rows, cold_rows, hist_lengths, out_grad, w_uvqk, w_out):
    grad_scale = 1.0 / math.sqrt(lax.axis_size("bal") * out_grad.shape[0])
    return put(*layer(
        lax.axis_size("table"), grad_scale, item_ids, hot_slot, hot_rows, cold_rows, hist_lengths, out_grad, w_uvqk, w_out
    ))


def solution(mesh):
    both = P(("table", "bal"), None)
    return jax.shard_map(
        per_device,
        mesh=mesh,
        in_specs=(P(("table", "bal")), P(), P(), P("table", None), P(), both, P(), P()),
        out_specs=(both, both, both),
        check_vma=False,
    )
```
